32 devices in a mesh: sector: 4 (over z), dir: 8 (over y, x, core).
Axes of the slice: x: 2, y: 2, z: 4, core: 2. Of those that a mesh axis runs over, the one named last changes fastest.
Arguments:
- fields: bfloat16 [1024, 128, 128], P(('sector', 'dir')), may hold values from -6 to 6
- aggregation: bfloat16 [64, 256], replicated, may hold values from -0.375 to 0.375
- operators: bfloat16 [64, 64, 64, 128], P(None, 'dir'), may hold values from -0.09375 to 0.09375
- disaggregation: bfloat16 [128, 128], replicated, may hold values from -0.5 to 0.5
- near_tile: int32 [16, 16], P('sector'), may hold values from 0 to 3
- near_operator: int32 [16, 16], P('sector'), may hold values from 0 to 63
- far_slot: int32 [16, 16], P('sector'), may hold values from 0 to 7, as said below
- far_operator: int32 [16, 16], P('sector'), may hold values from 0 to 63
- send_tiles: int32 [4, 4, 2], replicated, may hold values from 0 to 3, as said below
Outputs:
- scattered: bfloat16 [1024, 128, 128], P(('sector', 'dir'))
The draws below stay inside these ranges and needn't reach their ends.
Inputs may be any that keep to these rules, and one draw needn't show every extreme that they name: `send_tiles`: for every source and target sector the 2 entries are distinct tile numbers within the source sector. `far_slot`: entry c * 2 + j names slot j of the list that sector c keeps for the target tile's sector; c is never the target tile's own sector.
All inputs are finite; a program needn't handle non-finite values.
Results may differ from the reference program's by a relative error of at most 0.0058.
Values may be sent and summed in bfloat16 or wider, within the bound.
No kernel may reach another device: no remote copies, remote signals or barrier semaphores. Data moves between devices by JAX's collectives and lax.ppermute only.
A program may use at most 128 MiB of HBM per device.

```python
import jax
import jax.numpy as jnp
from jax import lax

Q = 128
K = 64
ILL = 64
TILE = 64
NOPS = 64
LNEAR = 16
LFAR = 16
CAP = 2
BOXES = 1024
TPS = 4
NTILES = 16


def draw_send_tiles(key, part):
    sectors = NTILES // TPS
    subkeys = jax.random.split(jax.random.fold_in(key, 11), sectors * sectors)
    orders = jax.vmap(lambda sub: jax.random.permutation(sub, TPS)[:CAP])(subkeys)
    return orders.reshape(sectors, sectors, CAP).astype(jnp.int32)


def draw_far_slot(key, part):
    sectors = NTILES // TPS
    base = jax.random.fold_in(key, 23)
    key_one, key_two, key_three = jax.random.split(base, 3)
    own_sector = (jnp.arange(NTILES, dtype=jnp.int32) // TPS)[:, None]
    first_pick = jax.random.randint(key_one, (NTILES, LFAR), 0, sectors - 1)
    second_pick = jax.random.randint(key_two, (NTILES, LFAR), 0, sectors - 1)
    distance = jnp.minimum(first_pick, second_pick) + 1
    source = (own_sector + distance) % sectors
    position = jax.random.randint(key_three, (NTILES, LFAR), 0, CAP)
    return (source * CAP + position).astype(jnp.int32)


def set_ends(values, rng, low, largest):
    longest = values.shape.index(max(values.shape))
    spots = []
    for shift in (0, 1):
        where = [jax.random.randint(jax.random.fold_in(rng, axis), (), 0, length) for axis, length in enumerate(values.shape)]
        where[longest] = (where[longest] + shift) % values.shape[longest]
        spots.append(tuple(where))
    return values.at[spots[0]].set(low).at[spots[1]].set(largest)


def steps_of(key, extent, pieces, low, largest):
    loudness, own = 1.0, jax.random.fold_in(key, 6)
    for dim, parts in pieces:
        heights = jnp.exp(jax.random.uniform(jax.random.fold_in(own, dim), (parts,), jnp.float32, low / len(pieces), largest / len(pieces)))
        loudness = loudness * jnp.repeat(heights, extent[dim] // parts).reshape([-1 if axis == dim else 1 for axis in range(len(extent))])
    return loudness


def scatter_about(key, shape, deviation, limit, cuts=(), kind=jnp.bfloat16):
    drawn = jax.random.normal(key, shape, jnp.float32) * deviation
    if len(cuts) > 0:
        drawn = steps_of(key, shape, cuts, -0.22, 0.18) * drawn
    return jnp.clip(drawn, min=-limit, max=limit).astype(kind)


def setup_inputs(seed: int = 0) -> dict:
    key_list = jax.random.split(jax.random.key(seed), 10)
    return {
        "fields": scatter_about(key_list[0], (BOXES, Q, 2 * ILL), 1.0, 6.0, ((0, 32),)),
        "aggregation": scatter_about(key_list[1], (K, 2 * Q), (2 * Q) ** -0.5, 0.375),
        "operators": scatter_about(key_list[2], (NOPS, K, TILE, 2 * TILE), (2 * TILE * (LNEAR + LFAR)) ** -0.5, 0.09375, ((1, 8),)),
        "disaggregation": scatter_about(key_list[3], (Q, 2 * K), (2 * K) ** -0.5, 0.5),
        "near_tile": set_ends(jax.random.randint(key_list[4], (NTILES, LNEAR), 0, TPS), jax.random.fold_in(key_list[4], 1), 0, TPS - 1).astype(jnp.int32),
        "near_operator": set_ends(jax.random.randint(key_list[5], (NTILES, LNEAR), 0, NOPS), jax.random.fold_in(key_list[5], 1), 0, NOPS - 1).astype(jnp.int32),
        "far_slot": draw_far_slot(jax.random.fold_in(key_list[9], 71), 0),
        "far_operator": set_ends(jax.random.randint(key_list[7], (NTILES, LFAR), 0, NOPS), jax.random.fold_in(key_list[7], 1), 0, NOPS - 1).astype(jnp.int32),
        "send_tiles": draw_send_tiles(jax.random.fold_in(key_list[9], 71), 0),
    }


def stacked(values, axis):
    halfway = values.shape[-1] // 2
    lower_rows = jnp.concatenate([-values[..., halfway:], values[..., :halfway]], axis=-1)
    return jnp.concatenate([values, lower_rows], axis=axis)


def reference(fields, aggregation, operators, disaggregation, near_tile, near_operator, far_slot, far_operator, send_tiles):
    agg_full = aggregation.astype(jnp.float32)
    dis_full = disaggregation.astype(jnp.float32)
    tile_fields = fields.reshape(NTILES, TILE, Q, 2 * ILL)

    def aggregate(block):
        return jnp.einsum('kq,bqc->bkc', agg_full, stacked(block, 1).astype(jnp.float32)).astype(jnp.bfloat16)

    outgoing = lax.map(aggregate, tile_fields)

    def translate(target):
        sector_now = target // TPS
        near_src = sector_now * TPS + near_tile[target]
        src_sector = far_slot[target] // CAP
        position = far_slot[target] % CAP
        far_src = src_sector * TPS + send_tiles[src_sector, sector_now, position]
        sources = jnp.concatenate([near_src, far_src]).astype(jnp.int32)
        chosen = jnp.concatenate([near_operator[target], far_operator[target]]).astype(jnp.int32)
        source_rows = stacked(outgoing[sources], 1).astype(jnp.float32)
        op_blocks = operators[chosen].astype(jnp.float32)
        return jnp.einsum('lkab,lbkc->akc', op_blocks, source_rows).astype(jnp.bfloat16)

    incoming = lax.map(translate, jnp.arange(NTILES, dtype=jnp.int32))

    def disaggregate(block):
        return jnp.einsum('qk,bkc->bqc', dis_full, stacked(block, 1).astype(jnp.float32)).astype(jnp.bfloat16)

    result = lax.map(disaggregate, incoming)
    return result.reshape(BOXES, Q, 2 * ILL)
```

```python
import jax
import jax.numpy as jnp
from jax import lax
from jax.experimental import pallas as pl
from jax.experimental.pallas import tpu as pltpu
from jax.sharding import PartitionSpec as P

CHUNKS = 1
MIB = 1024 * 1024


def turned(values):
    half = values.shape[-1] // 2
    lane = lax.broadcasted_iota(jnp.int32, values.shape, values.ndim - 1)
    moved = pltpu.roll(values, half, values.ndim - 1)
    return jnp.where(lane < half, -moved, moved)


def stack_rows(values):
    wide = values.astype(jnp.float32)
    return jnp.concatenate([wide, turned(wide)], axis=0).astype(jnp.bfloat16)


def vmem(count):
    return [pl.BlockSpec(memory_space=pltpu.VMEM)] * count


def smem(count):
    return [pl.BlockSpec(memory_space=pltpu.SMEM)] * count


def aggregate(fields, aggregation, devices, chunks):
    boxes, unknowns, columns = fields.shape
    all_dirs = aggregation.shape[0]
    part = all_dirs // devices // chunks

    def kernel(fields_ref, agg_ref, *refs):
        outs, scratch = refs[:chunks], refs[chunks]
        matrix = jnp.concatenate([agg_ref[:, :unknowns], agg_ref[:, unknowns:]], axis=0)
        for box in range(boxes):
            both = jnp.dot(matrix, fields_ref[box], preferred_element_type=jnp.float32)
            scratch[box * all_dirs : (box + 1) * all_dirs, :] = both[:all_dirs] + turned(both[all_dirs:])
        for direction in range(all_dirs):
            device, place = divmod(direction, part * chunks)
            chunk, inner = divmod(place, part)
            rows = scratch[pl.ds(direction, boxes, stride=all_dirs), :]
            outs[chunk][device, inner] = rows.astype(jnp.bfloat16)

    return pl.pallas_call(
        kernel,
        out_shape=[jax.ShapeDtypeStruct((devices, part, boxes, columns), jnp.bfloat16)] * chunks,
        in_specs=vmem(2),
        out_specs=vmem(chunks),
        scratch_shapes=[pltpu.VMEM((boxes * all_dirs, columns), jnp.float32)],
        name="aggregate",
    )(fields, aggregation)


def pick(slab, listing, where, partners, cap, per_tile):
    devices, part, boxes, columns = slab.shape

    def kernel(listing_ref, where_ref, slab_ref, *outs):
        for index in range(partners):
            other = where_ref[0] ^ (index + 1)
            for slot in range(cap):
                tile = listing_ref[where_ref[0], other, slot]
                outs[index][slot] = slab_ref[pl.ds(tile * per_tile, per_tile)]

    shape = jax.ShapeDtypeStruct((cap, per_tile, part, boxes, columns), jnp.bfloat16)
    return pl.pallas_call(
        kernel,
        out_shape=[shape] * partners,
        in_specs=smem(2) + vmem(1),
        out_specs=vmem(partners),
        name="pick",
    )(listing, where, slab)


def build(operators, near_tile, near_operator, far_slot, far_operator, where, partners, cap):
    count, dirs, rows, wide = operators.shape
    tiles, entries = near_tile.shape
    far_entries = far_slot.shape[1]
    slots = partners * cap
    group = min(4, tiles)

    def kernel(near_tile_ref, near_op_ref, far_slot_ref, far_op_ref, where_ref, op_ref, near_out, far_out, *scratch):
        near_sum, far_sum = scratch[:group], scratch[group:]
        for base in range(0, tiles, group):
            for ref in scratch:
                ref[...] = jnp.zeros_like(ref)

            def add(entry, _):
                for t in range(group):
                    source = near_tile_ref[base + t, entry]
                    block = op_ref[near_op_ref[base + t, entry]]
                    near_sum[t][source] += block.astype(jnp.float32)
                return 0

            def add_far(entry, _):
                for t in range(group):
                    place = far_slot_ref[base + t, entry]
                    sector = (place // cap) ^ where_ref[0]
                    slot = (sector - 1) * cap + place % cap
                    block = op_ref[far_op_ref[base + t, entry]]
                    far_sum[t][slot] += block.astype(jnp.float32)
                return 0

            lax.fori_loop(0, entries, add, 0)
            lax.fori_loop(0, far_entries, add_far, 0)
            for t in range(group):
                at = pl.ds((base + t) * rows, rows)
                near_out[:, at, :] = near_sum[t][...].astype(jnp.bfloat16)
                far_out[:, at, :] = far_sum[t][...].astype(jnp.bfloat16)

    return pl.pallas_call(
        kernel,
        grid=(dirs,),
        out_shape=[
            jax.ShapeDtypeStruct((dirs, tiles, tiles * rows, wide), jnp.bfloat16),
            jax.ShapeDtypeStruct((dirs, slots, tiles * rows, wide), jnp.bfloat16),
        ],
        in_specs=smem(5) + [pl.BlockSpec((count, None, rows, wide), lambda k: (0, k, 0, 0))],
        out_specs=[
            pl.BlockSpec((None, tiles, tiles * rows, wide), lambda k: (k, 0, 0, 0)),
            pl.BlockSpec((None, slots, tiles * rows, wide), lambda k: (k, 0, 0, 0)),
        ],
        scratch_shapes=[pltpu.VMEM((tiles, rows, wide), jnp.float32)] * group
        + [pltpu.VMEM((slots, rows, wide), jnp.float32)] * group,
        compiler_params=pltpu.CompilerParams(vmem_limit_bytes=40 * MIB),
        cost_estimate=pl.CostEstimate(
            flops=20 * dirs * tiles * (entries + far_entries) * rows * wide,
            bytes_accessed=2 * operators.size + 2 * dirs * (tiles + slots) * tiles * rows * wide,
            transcendentals=0,
        ),
        name="build",
    )(near_tile, near_operator, far_slot, far_operator, where, operators)


def wide_block(block_ref, slots):
    return jnp.concatenate([block_ref[slot] for slot in range(slots)], axis=1)


def near_product(blocks, slab, first, per_tile):
    _, tiles, rows, wide = blocks.shape
    devices, part, boxes, columns = slab.shape

    def kernel(block_ref, slab_ref, out_ref):
        sources = []
        for tile in range(tiles):
            pieces = [slab_ref[tile * per_tile + piece] for piece in range(per_tile)]
            sources.append(stack_rows(jnp.concatenate(pieces, axis=0)))
        out_ref[...] = jnp.dot(
            wide_block(block_ref, tiles), jnp.concatenate(sources, axis=0), preferred_element_type=jnp.float32
        )

    return pl.pallas_call(
        kernel,
        grid=(part,),
        out_shape=jax.ShapeDtypeStruct((part, rows, columns), jnp.float32),
        in_specs=[
            pl.BlockSpec((None, tiles, rows, wide), lambda k: (first + k, 0, 0, 0)),
            pl.BlockSpec((devices, None, boxes, columns), lambda k: (0, k, 0, 0)),
        ],
        out_specs=pl.BlockSpec((None, rows, columns), lambda k: (k, 0, 0)),
        compiler_params=pltpu.CompilerParams(vmem_limit_bytes=40 * MIB),
        cost_estimate=pl.CostEstimate(
            flops=8 * part * rows * tiles * wide * columns,
            bytes_accessed=2 * blocks.size // blocks.shape[0] * part + 2 * slab.size,
            transcendentals=0,
        ),
        name="near_product",
    )(blocks, slab)


def far_product(blocks, arrived, near, first, devices, per_tile):
    _, slots, rows, wide = blocks.shape
    cap, _, part, boxes, columns = arrived[0].shape
    partners = len(arrived)

    def kernel(block_ref, near_ref, *refs):
        out_ref = refs[partners]
        sources = []
        for index in range(partners):
            for slot in range(cap):
                pieces = [refs[index][slot, piece] for piece in range(per_tile)]
                sources.append(stack_rows(jnp.concatenate(pieces, axis=0)))
        total = near_ref[...] + jnp.dot(
            wide_block(block_ref, slots), jnp.concatenate(sources, axis=0), preferred_element_type=jnp.float32
        )
        total = total.astype(jnp.bfloat16)
        for device in range(devices):
            out_ref[device] = total[device * boxes : (device + 1) * boxes]

    return pl.pallas_call(
        kernel,
        grid=(part,),
        out_shape=jax.ShapeDtypeStruct((devices, part, boxes, columns), jnp.bfloat16),
        in_specs=[
            pl.BlockSpec((None, slots, rows, wide), lambda k: (first + k, 0, 0, 0)),
            pl.BlockSpec((None, rows, columns), lambda k: (k, 0, 0)),
        ]
        + [pl.BlockSpec((cap, per_tile, None, boxes, columns), lambda k: (0, 0, k, 0, 0))] * partners,
        out_specs=pl.BlockSpec((devices, None, boxes, columns), lambda k: (0, k, 0, 0)),
        compiler_params=pltpu.CompilerParams(vmem_limit_bytes=40 * MIB),
        name="far_product",
    )(blocks, near, *arrived)


def disaggregate(returned, disaggregation):
    devices, part, boxes, columns = returned[0].shape
    chunks = len(returned)
    unknowns = disaggregation.shape[0]
    all_dirs = disaggregation.shape[1] // 2

    def kernel(dis_ref, *refs):
        out_ref, scratch = refs[chunks], refs[chunks + 1]
        for direction in range(all_dirs):
            device, place = divmod(direction, part * chunks)
            chunk, inner = divmod(place, part)
            scratch[direction * boxes : (direction + 1) * boxes, :] = refs[chunk][device, inner].astype(jnp.float32)
        matrix = dis_ref[...]
        for box in range(boxes):
            rows = stack_rows(scratch[pl.ds(box, all_dirs, stride=boxes), :])
            out_ref[box] = jnp.dot(matrix, rows, preferred_element_type=jnp.float32).astype(jnp.bfloat16)

    return pl.pallas_call(
        kernel,
        out_shape=jax.ShapeDtypeStruct((boxes, unknowns, columns), jnp.bfloat16),
        in_specs=vmem(1 + chunks),
        out_specs=pl.BlockSpec(memory_space=pltpu.VMEM),
        scratch_shapes=[pltpu.VMEM((all_dirs * boxes, columns), jnp.float32)],
        name="disaggregate",
    )(disaggregation, *returned)


def make_local(sectors, devices):
    def local(
        fields,
        aggregation,
        operators,
        disaggregation,
        near_tile,
        near_operator,
        far_slot,
        far_operator,
        send_tiles,
    ):
        dirs_here = operators.shape[1]
        per_tile = operators.shape[2] // fields.shape[0]
        cap = send_tiles.shape[2]
        chunks = min(CHUNKS, dirs_here)
        part = dirs_here // chunks
        where = lax.axis_index("sector").astype(jnp.int32).reshape(1)
        outgoing = aggregate(fields, aggregation, devices, chunks)
        near_blocks, far_blocks = build(
            operators, near_tile, near_operator, far_slot, far_operator, where, sectors - 1, cap
        )
        returned = []
        for chunk in range(chunks):
            slab = lax.all_to_all(outgoing[chunk], "dir", 0, 0, tiled=True)
            leaving = pick(slab, send_tiles, where, sectors - 1, cap, per_tile)
            arrived = [
                lax.ppermute(leaving[index], "sector", [(i, i ^ (index + 1)) for i in range(sectors)])
                for index in range(sectors - 1)
            ]
            near = near_product(near_blocks, slab, chunk * part, per_tile)
            incoming = far_product(far_blocks, arrived, near, chunk * part, devices, per_tile)
            returned.append(lax.all_to_all(incoming, "dir", 0, 0, tiled=True))
        return disaggregate(returned, disaggregation)

    return local


def solution(mesh):
    placed = (
        P(("sector", "dir"), None, None),
        P(),
        P(None, "dir", None, None),
        P(),
        P("sector", None),
        P("sector", None),
        P("sector", None),
        P("sector", None),
        P(),
    )
    return jax.shard_map(
        make_local(mesh.shape["sector"], mesh.shape["dir"]),
        mesh=mesh,
        in_specs=placed,
        out_specs=P(("sector", "dir"), None, None),
        check_vma=False,
    )
```

```python
import jax
import jax.numpy as jnp
from jax import lax
from jax.experimental import pallas as pl
from jax.experimental.pallas import tpu as pltpu
from jax.sharding import PartitionSpec as P

MIB = 1024 * 1024
STEP_DIRS = 2
AGG_MIB = 20
OP_CUTS = 4
LITTLE = pl.CostEstimate(flops=1, bytes_accessed=1, transcendentals=0)


def turned(values):
    half = values.shape[-1] // 2
    lane = lax.broadcasted_iota(jnp.int32, values.shape, values.ndim - 1)
    moved = pltpu.roll(values, half, values.ndim - 1)
    return jnp.where(lane < half, -moved, moved)


def stack_rows(values):
    wide = values.astype(jnp.float32)
    return jnp.concatenate([wide, turned(wide)], axis=0).astype(jnp.bfloat16)


def vmem(count):
    return [pl.BlockSpec(memory_space=pltpu.VMEM)] * count


def smem(count):
    return [pl.BlockSpec(memory_space=pltpu.SMEM)] * count


def aggregate(fields, aggregation, place, devices):
    boxes, unknowns, columns = fields.shape
    all_dirs = aggregation.shape[0]
    part = all_dirs // devices

    def kernel(place_ref, fields_ref, agg_ref, *refs):
        outs, scratch = refs[:devices], refs[devices]
        matrix = jnp.concatenate([agg_ref[:, :unknowns], agg_ref[:, unknowns:]], axis=0)
        for box in range(boxes):
            both = jnp.dot(matrix, fields_ref[box], preferred_element_type=jnp.float32)
            scratch[box * all_dirs : (box + 1) * all_dirs, :] = both[:all_dirs] + turned(both[all_dirs:])
        for step in range(devices):
            first = (place_ref[0] ^ step) * part
            for inner in range(part):
                rows = scratch[pl.ds(first + inner, boxes, stride=all_dirs), :]
                outs[step][inner] = rows.astype(jnp.bfloat16)

    return pl.pallas_call(
        kernel,
        out_shape=[jax.ShapeDtypeStruct((part, boxes, columns), jnp.bfloat16)] * devices,
        in_specs=smem(1) + vmem(2),
        out_specs=vmem(devices),
        scratch_shapes=[pltpu.VMEM((boxes * all_dirs, columns), jnp.float32)],
        compiler_params=pltpu.CompilerParams(vmem_limit_bytes=AGG_MIB * MIB),
        cost_estimate=LITTLE,
        name="aggregate",
    )(place, fields, aggregation)


def pick(pieces, listing, where, place, partners, per_tile):
    devices = len(pieces)
    dirs, boxes, columns = pieces[0].shape
    cap = listing.shape[1]

    def kernel(listing_ref, where_ref, place_ref, *refs):
        slab_ref, outs = refs[devices], refs[devices + 1 :]
        for step in range(devices):
            slab_ref[place_ref[0] ^ step] = refs[step][...]
        for index in range(partners):
            other = where_ref[0] ^ (index + 1)
            for slot in range(cap):
                tile = listing_ref[where_ref[0], slot, other]
                outs[index][slot] = slab_ref[pl.ds(tile * per_tile, per_tile)]

    shapes = [(devices, dirs, boxes, columns)] + [(cap, per_tile, dirs, boxes, columns)] * partners
    outs = pl.pallas_call(
        kernel,
        grid=(1,),
        out_shape=[jax.ShapeDtypeStruct(shape, jnp.bfloat16) for shape in shapes],
        in_specs=smem(3) + [pl.BlockSpec(piece.shape, lambda i: (0, 0, 0)) for piece in pieces],
        out_specs=[pl.BlockSpec(shape, lambda i, n=len(shape): (0,) * n) for shape in shapes],
        compiler_params=pltpu.CompilerParams(vmem_limit_bytes=20 * MIB),
        cost_estimate=LITTLE,
        name="pick",
    )(listing, where, place, *pieces)
    return outs[0], outs[1:]


def build(operators, near_tile, near_operator, far_slot, far_operator, where, partners, cap):
    count, dirs, rows, wide = operators.shape
    tiles, entries = near_tile.shape
    far_entries = far_slot.shape[1]
    slots = partners * cap
    group = min(4, tiles)
    total = entries + far_entries
    cuts = OP_CUTS if count % OP_CUTS == 0 else 1
    size = count // cuts
    tables = (near_tile, near_operator, far_slot, far_operator)

    def kernel(where_ref, *refs):
        sources, op_hbm, near_out, far_out = refs[:4], refs[4], refs[5], refs[6]
        listed, slot_table, op_table, ops, table_sem, op_sem = refs[7:11], refs[11], refs[12], refs[13], refs[14], refs[15]
        sums = refs[16:]
        near_sum, far_sum = sums[:group], sums[group:]
        now = pl.program_id(0)

        def table_copy(index):
            return pltpu.make_async_copy(sources[index], listed[index], table_sem.at[index])

        def op_copy(direction, cut):
            at = pl.ds(cut * size, size)
            return pltpu.make_async_copy(op_hbm.at[at, direction], ops.at[direction, at], op_sem.at[direction, cut])

        @pl.when(now == 0)
        def _():
            for index in range(4):
                table_copy(index).start()
            for direction in range(dirs):
                for cut in range(cuts):
                    op_copy(direction, cut).start()
            for index in range(4):
                table_copy(index).wait()
            for tile in range(tiles):

                def fill(entry, _):
                    slot_table[tile * total + entry] = listed[0][tile, entry]
                    op_table[tile * total + entry] = listed[1][tile, entry]
                    return 0

                def fill_far(entry, _):
                    place = listed[2][tile, entry]
                    sector = lax.div(place, cap)
                    slot = ((sector ^ where_ref[0]) - 1) * cap + place - sector * cap
                    slot_table[tile * total + entries + entry] = slot
                    op_table[tile * total + entries + entry] = listed[3][tile, entry]
                    return 0

                lax.fori_loop(0, entries, fill, 0, unroll=4)
                lax.fori_loop(0, far_entries, fill_far, 0, unroll=4)

        for cut in range(cuts):
            op_copy(now, cut).wait()
        for base in range(0, tiles, group):
            for ref in sums:
                ref[...] = jnp.zeros_like(ref)
            for entry in range(total):
                for t in range(group):
                    at = (base + t) * total + entry
                    kept = near_sum[t] if entry < entries else far_sum[t]
                    kept[slot_table[at]] += ops[now, op_table[at]].astype(jnp.float32)
            for t in range(group):
                at = pl.ds((base + t) * rows, rows)
                near_out[:, at, :] = near_sum[t][...].astype(jnp.bfloat16)
                far_out[:, at, :] = far_sum[t][...].astype(jnp.bfloat16)

    need = 2 * operators.size + 4 * group * (tiles + slots) * rows * wide + 8 * (tiles + slots) * tiles * rows * wide
    return pl.pallas_call(
        kernel,
        grid=(dirs,),
        out_shape=[
            jax.ShapeDtypeStruct((dirs, tiles, tiles * rows, wide), jnp.bfloat16),
            jax.ShapeDtypeStruct((dirs, slots, tiles * rows, wide), jnp.bfloat16),
        ],
        in_specs=smem(1) + [pl.BlockSpec(memory_space=pltpu.HBM)] * 5,
        out_specs=[
            pl.BlockSpec((None, tiles, tiles * rows, wide), lambda k: (k, 0, 0, 0)),
            pl.BlockSpec((None, slots, tiles * rows, wide), lambda k: (k, 0, 0, 0)),
        ],
        scratch_shapes=[pltpu.SMEM(table.shape, jnp.int32) for table in tables]
        + [pltpu.SMEM((tiles * total,), jnp.int32)] * 2
        + [
            pltpu.VMEM((dirs, count, rows, wide), jnp.bfloat16),
            pltpu.SemaphoreType.DMA((4,)),
            pltpu.SemaphoreType.DMA((dirs, cuts)),
        ]
        + [pltpu.VMEM((tiles, rows, wide), jnp.float32)] * group
        + [pltpu.VMEM((slots, rows, wide), jnp.float32)] * group,
        compiler_params=pltpu.CompilerParams(vmem_limit_bytes=need + 4 * MIB),
        cost_estimate=LITTLE,
        name="build",
    )(where, *tables, operators)


def wide_block(block_ref, slots):
    return jnp.concatenate([block_ref[slot] for slot in range(slots)], axis=1)


def near_product(blocks, slab, per_tile):
    dirs, tiles, rows, wide = blocks.shape
    devices, _, boxes, columns = slab.shape
    group = STEP_DIRS if dirs % STEP_DIRS == 0 else 1

    def kernel(block_ref, slab_ref, out_ref):
        for inner in range(group):
            sources = []
            for tile in range(tiles):
                pieces = [slab_ref[tile * per_tile + piece, inner] for piece in range(per_tile)]
                sources.append(stack_rows(jnp.concatenate(pieces, axis=0)))
            out_ref[inner] = jnp.dot(
                wide_block(block_ref.at[inner], tiles),
                jnp.concatenate(sources, axis=0),
                preferred_element_type=jnp.float32,
            )

    return pl.pallas_call(
        kernel,
        grid=(dirs // group,),
        out_shape=jax.ShapeDtypeStruct((dirs, rows, columns), jnp.float32),
        in_specs=[
            pl.BlockSpec((group, tiles, rows, wide), lambda k: (k, 0, 0, 0)),
            pl.BlockSpec((devices, group, boxes, columns), lambda k: (0, k, 0, 0)),
        ],
        out_specs=pl.BlockSpec((group, rows, columns), lambda k: (k, 0, 0)),
        compiler_params=pltpu.CompilerParams(vmem_limit_bytes=40 * MIB),
        cost_estimate=LITTLE,
        name="near_product",
    )(blocks, slab)


def far_product(blocks, arrived, first, before, place, devices, per_tile):
    dirs, _, rows, wide = blocks.shape
    cap, _, _, boxes, columns = arrived[0].shape
    count = len(arrived)
    slots = count * cap
    last = place is not None
    group = STEP_DIRS if dirs % STEP_DIRS == 0 else 1

    def kernel(block_ref, before_ref, *refs):
        taken, outs = refs[:count], refs[count:]
        step = pl.program_id(0)
        for inner in range(group):
            sources = []
            for index in range(count):
                for slot in range(cap):
                    pieces = [taken[index][slot, piece, inner] for piece in range(per_tile)]
                    sources.append(stack_rows(jnp.concatenate(pieces, axis=0)))
            total = before_ref[inner] + jnp.dot(
                wide_block(block_ref.at[inner], slots),
                jnp.concatenate(sources, axis=0),
                preferred_element_type=jnp.float32,
            )
            if last:
                total_ref = outs[-1]
                total_ref[inner] = total
                for index in range(devices):
                    at = pl.multiple_of((outs[-2][0] ^ index) * boxes, boxes)
                    outs[index][step * group + inner] = total_ref[inner, pl.ds(at, boxes), :].astype(jnp.bfloat16)
            else:
                outs[0][inner] = total

    def kernel_last(place_ref, block_ref, before_ref, *refs):
        kernel(block_ref, before_ref, *refs[: count + devices], place_ref, refs[count + devices])

    in_specs = [
        pl.BlockSpec((group, slots, rows, wide), lambda k: (k, first, 0, 0)),
        pl.BlockSpec((group, rows, columns), lambda k: (k, 0, 0)),
    ] + [pl.BlockSpec((cap, per_tile, group, boxes, columns), lambda k: (0, 0, k, 0, 0))] * count
    operands = [blocks, before, *arrived]
    if last:
        in_specs = smem(1) + in_specs
        operands = [place] + operands
        out_shape = [jax.ShapeDtypeStruct((dirs, boxes, columns), jnp.bfloat16)] * devices
        out_specs = [pl.BlockSpec((dirs, boxes, columns), lambda k: (0, 0, 0))] * devices
        scratch = [pltpu.VMEM((group, rows, columns), jnp.float32)]
    else:
        out_shape = [jax.ShapeDtypeStruct((dirs, rows, columns), jnp.float32)]
        out_specs = [pl.BlockSpec((group, rows, columns), lambda k: (k, 0, 0))]
        scratch = []
    return pl.pallas_call(
        kernel_last if last else kernel,
        grid=(dirs // group,),
        out_shape=out_shape,
        in_specs=in_specs,
        out_specs=out_specs,
        scratch_shapes=scratch,
        compiler_params=pltpu.CompilerParams(vmem_limit_bytes=40 * MIB),
        cost_estimate=LITTLE,
        name="far_last" if last else "far_first",
    )(*operands)


def disaggregate(returned, disaggregation, place):
    dirs, boxes, columns = returned[0].shape
    devices = len(returned)
    unknowns = disaggregation.shape[0]
    all_dirs = disaggregation.shape[1] // 2
    step = boxes // 2

    def kernel(place_ref, dis_ref, *refs):
        out_ref, scratch = refs[devices], refs[devices + 1]
        for index in range(devices):
            first = (place_ref[0] ^ index) * dirs
            for inner in range(dirs):
                at = pl.multiple_of((first + inner) * step, step)
                scratch[pl.ds(at, step), :] = refs[index][inner].astype(jnp.float32)
        matrix = dis_ref[...]
        for box in range(step):
            rows = stack_rows(scratch[pl.ds(box, all_dirs, stride=step), :])
            out_ref[box] = jnp.dot(matrix, rows, preferred_element_type=jnp.float32).astype(jnp.bfloat16)

    return pl.pallas_call(
        kernel,
        grid=(boxes // step,),
        out_shape=jax.ShapeDtypeStruct((boxes, unknowns, columns), jnp.bfloat16),
        in_specs=smem(1)
        + [pl.BlockSpec(disaggregation.shape, lambda i: (0, 0))]
        + [pl.BlockSpec((dirs, step, columns), lambda i: (0, i, 0))] * devices,
        out_specs=pl.BlockSpec((step, unknowns, columns), lambda i: (i, 0, 0)),
        scratch_shapes=[pltpu.VMEM((all_dirs * step, columns), jnp.float32)],
        compiler_params=pltpu.CompilerParams(vmem_limit_bytes=20 * MIB),
        cost_estimate=LITTLE,
        name="disaggregate",
    )(place, disaggregation, *returned)


def crossed(pieces, axis):
    count = len(pieces)
    moved = [lax.ppermute(pieces[step], axis, [(i, i ^ step) for i in range(count)]) for step in range(1, count)]
    return [pieces[0]] + moved


def make_local(sectors, devices):
    partners = sectors - 1
    barrier = lax.optimization_barrier

    def local(
        fields,
        aggregation,
        operators,
        disaggregation,
        near_tile,
        near_operator,
        far_slot,
        far_operator,
        send_tiles,
    ):
        per_tile = operators.shape[2] // fields.shape[0]
        cap = send_tiles.shape[2]
        where = lax.axis_index("sector").astype(jnp.int32).reshape(1)
        place = lax.axis_index("dir").astype(jnp.int32).reshape(1)
        listing = jnp.swapaxes(send_tiles, 1, 2)
        outgoing = aggregate(fields, aggregation, place, devices)
        pieces = crossed(outgoing, "dir")
        slab, leaving = pick(pieces, listing, where, place, partners, per_tile)
        leaving, tile_index = barrier((leaving, near_tile))
        arrived = crossed([leaving[0], *leaving], "sector")[1:]
        near_blocks, far_blocks = build(
            operators, tile_index, near_operator, far_slot, far_operator, where, partners, cap
        )
        total = near_product(near_blocks, slab, per_tile)
        total = far_product(far_blocks, arrived[:-1], 0, total, None, devices, per_tile)[0]
        incoming = far_product(far_blocks, arrived[-1:], partners - 1, total, place, devices, per_tile)
        returned = crossed(incoming, "dir")
        return disaggregate(returned, disaggregation, place)

    return local


def solution(mesh):
    placed = (
        P(("sector", "dir"), None, None),
        P(),
        P(None, "dir", None, None),
        P(),
        P("sector", None),
        P("sector", None),
        P("sector", None),
        P("sector", None),
        P(),
    )
    return jax.shard_map(
        make_local(mesh.shape["sector"], mesh.shape["dir"]),
        mesh=mesh,
        in_specs=placed,
        out_specs=P(("sector", "dir"), None, None),
        check_vma=False,
    )
```

```python
import jax
import jax.numpy as jnp
from jax import lax
from jax.experimental import pallas as pl
from jax.experimental.pallas import tpu as pltpu
from jax.sharding import PartitionSpec as P

MIB = 1024 * 1024
STEP_DIRS = 2
AGG_MIB = 20
OP_CUTS = 4
LITTLE = pl.CostEstimate(flops=1, bytes_accessed=1, transcendentals=0)


def order(count):
    return sorted(range(count), key=lambda step: (step == 0, -bin(step >> 1).count("1"), -(step & 1), step))


def turned(values):
    half = values.shape[-1] // 2
    lane = lax.broadcasted_iota(jnp.int32, values.shape, values.ndim - 1)
    moved = pltpu.roll(values, half, values.ndim - 1)
    return jnp.where(lane < half, -moved, moved)


def stack_rows(values):
    wide = values.astype(jnp.float32)
    return jnp.concatenate([wide, turned(wide)], axis=0).astype(jnp.bfloat16)


def vmem(count):
    return [pl.BlockSpec(memory_space=pltpu.VMEM)] * count


def smem(count):
    return [pl.BlockSpec(memory_space=pltpu.SMEM)] * count


def aggregate(fields, aggregation, place, devices):
    boxes, unknowns, columns = fields.shape
    all_dirs = aggregation.shape[0]
    part = all_dirs // devices

    def kernel(place_ref, fields_ref, agg_ref, *refs):
        outs, scratch = refs[:devices], refs[devices]
        matrix = jnp.concatenate([agg_ref[:, :unknowns], agg_ref[:, unknowns:]], axis=0)
        for box in range(boxes):
            both = jnp.dot(matrix, fields_ref[box], preferred_element_type=jnp.float32)
            scratch[box * all_dirs : (box + 1) * all_dirs, :] = both[:all_dirs] + turned(both[all_dirs:])
        for step in range(devices):
            first = (place_ref[0] ^ step) * part
            for inner in range(part):
                rows = scratch[pl.ds(first + inner, boxes, stride=all_dirs), :]
                outs[step][inner] = rows.astype(jnp.bfloat16)

    return pl.pallas_call(
        kernel,
        out_shape=[jax.ShapeDtypeStruct((part, boxes, columns), jnp.bfloat16)] * devices,
        in_specs=smem(1) + vmem(2),
        out_specs=vmem(devices),
        scratch_shapes=[pltpu.VMEM((boxes * all_dirs, columns), jnp.float32)],
        compiler_params=pltpu.CompilerParams(vmem_limit_bytes=AGG_MIB * MIB),
        cost_estimate=LITTLE,
        name="aggregate",
    )(place, fields, aggregation)


def pick(pieces, listing, where, place, partners, per_tile):
    devices = len(pieces)
    dirs, boxes, columns = pieces[0].shape
    cap = listing.shape[0]

    def kernel(listing_ref, where_ref, place_ref, *refs):
        slab_ref, outs = refs[devices], refs[devices + 1 :]
        for index, step in enumerate(order(devices)):
            slab_ref[place_ref[0] ^ step] = refs[index][...]
        for index in range(partners):
            other = where_ref[0] ^ (index + 1)
            for slot in range(cap):
                tile = listing_ref[slot, other]
                outs[index][slot] = slab_ref[pl.ds(tile * per_tile, per_tile)]

    shapes = [(devices, dirs, boxes, columns)] + [(cap, per_tile, dirs, boxes, columns)] * partners
    outs = pl.pallas_call(
        kernel,
        grid=(1,),
        out_shape=[jax.ShapeDtypeStruct(shape, jnp.bfloat16) for shape in shapes],
        in_specs=smem(3) + [pl.BlockSpec(piece.shape, lambda i: (0, 0, 0)) for piece in pieces],
        out_specs=[pl.BlockSpec(shape, lambda i, n=len(shape): (0,) * n) for shape in shapes],
        compiler_params=pltpu.CompilerParams(vmem_limit_bytes=20 * MIB),
        cost_estimate=LITTLE,
        name="pick",
    )(listing, where, place, *[pieces[step] for step in order(devices)])
    return outs[0], outs[1:]


def build(operators, near_tile, near_operator, far_slot, far_operator, where, partners, cap):
    count, dirs, rows, wide = operators.shape
    tiles, entries = near_tile.shape
    far_entries = far_slot.shape[1]
    slots = partners * cap
    group = min(4, tiles)
    total = entries + far_entries
    cuts = OP_CUTS if count % OP_CUTS == 0 else 1
    size = count // cuts
    tables = (near_tile, near_operator, far_slot, far_operator)

    def kernel(where_ref, *refs):
        sources, op_hbm, near_out, far_out = refs[:4], refs[4], refs[5], refs[6]
        listed, slot_table, op_table, ops, table_sem, op_sem = refs[7:11], refs[11], refs[12], refs[13], refs[14], refs[15]
        sums = refs[16:]
        near_sum, far_sum = sums[:group], sums[group:]
        now = pl.program_id(0)

        def table_copy(index):
            return pltpu.make_async_copy(sources[index], listed[index], table_sem.at[index])

        def op_copy(direction, cut):
            at = pl.ds(cut * size, size)
            return pltpu.make_async_copy(op_hbm.at[at, direction], ops.at[direction, at], op_sem.at[direction, cut])

        @pl.when(now == 0)
        def _():
            for index in range(4):
                table_copy(index).start()
            for direction in range(dirs):
                for cut in range(cuts):
                    op_copy(direction, cut).start()
            for index in range(4):
                table_copy(index).wait()
            for tile in range(tiles):

                def fill(entry, _):
                    slot_table[tile * total + entry] = listed[0][tile, entry]
                    op_table[tile * total + entry] = listed[1][tile, entry]
                    return 0

                def fill_far(entry, _):
                    place = listed[2][tile, entry]
                    sector = lax.div(place, cap)
                    step = sector ^ where_ref[0]
                    slot = (jnp.where(step <= 2, 2 - step, step - 1)) * cap + place - sector * cap
                    slot_table[tile * total + entries + entry] = slot
                    op_table[tile * total + entries + entry] = listed[3][tile, entry]
                    return 0

                lax.fori_loop(0, entries, fill, 0, unroll=4)
                lax.fori_loop(0, far_entries, fill_far, 0, unroll=4)

        for cut in range(cuts):
            op_copy(now, cut).wait()
        for base in range(0, tiles, group):
            for ref in sums:
                ref[...] = jnp.zeros_like(ref)
            for entry in range(total):
                for t in range(group):
                    at = (base + t) * total + entry
                    kept = near_sum[t] if entry < entries else far_sum[t]
                    kept[slot_table[at]] += ops[now, op_table[at]].astype(jnp.float32)
            for t in range(group):
                at = pl.ds((base + t) * rows, rows)
                near_out[:, at, :] = near_sum[t][...].astype(jnp.bfloat16)
                far_out[:, at, :] = far_sum[t][...].astype(jnp.bfloat16)

    need = 2 * operators.size + 4 * group * (tiles + slots) * rows * wide + 8 * (tiles + slots) * tiles * rows * wide
    return pl.pallas_call(
        kernel,
        grid=(dirs,),
        out_shape=[
            jax.ShapeDtypeStruct((dirs, tiles, tiles * rows, wide), jnp.bfloat16),
            jax.ShapeDtypeStruct((dirs, slots, tiles * rows, wide), jnp.bfloat16),
        ],
        in_specs=smem(1) + [pl.BlockSpec(memory_space=pltpu.HBM)] * 5,
        out_specs=[
            pl.BlockSpec((None, tiles, tiles * rows, wide), lambda k: (k, 0, 0, 0)),
            pl.BlockSpec((None, slots, tiles * rows, wide), lambda k: (k, 0, 0, 0)),
        ],
        scratch_shapes=[pltpu.SMEM(table.shape, jnp.int32) for table in tables]
        + [pltpu.SMEM((tiles * total,), jnp.int32)] * 2
        + [
            pltpu.VMEM((dirs, count, rows, wide), jnp.bfloat16),
            pltpu.SemaphoreType.DMA((4,)),
            pltpu.SemaphoreType.DMA((dirs, cuts)),
        ]
        + [pltpu.VMEM((tiles, rows, wide), jnp.float32)] * group
        + [pltpu.VMEM((slots, rows, wide), jnp.float32)] * group,
        compiler_params=pltpu.CompilerParams(vmem_limit_bytes=need + 4 * MIB),
        cost_estimate=LITTLE,
        name="build",
    )(where, *tables, operators)


def wide_block(block_ref, slots):
    return jnp.concatenate([block_ref[slot] for slot in range(slots)], axis=1)


def near_product(blocks, slab, per_tile):
    dirs, tiles, rows, wide = blocks.shape
    devices, _, boxes, columns = slab.shape
    group = STEP_DIRS if dirs % STEP_DIRS == 0 else 1

    def kernel(block_ref, slab_ref, out_ref):
        for inner in range(group):
            sources = []
            for tile in range(tiles):
                pieces = [slab_ref[tile * per_tile + piece, inner] for piece in range(per_tile)]
                sources.append(stack_rows(jnp.concatenate(pieces, axis=0)))
            out_ref[inner] = jnp.dot(
                wide_block(block_ref.at[inner], tiles),
                jnp.concatenate(sources, axis=0),
                preferred_element_type=jnp.float32,
            )

    return pl.pallas_call(
        kernel,
        grid=(dirs // group,),
        out_shape=jax.ShapeDtypeStruct((dirs, rows, columns), jnp.float32),
        in_specs=[
            pl.BlockSpec((group, tiles, rows, wide), lambda k: (k, 0, 0, 0)),
            pl.BlockSpec((devices, group, boxes, columns), lambda k: (0, k, 0, 0)),
        ],
        out_specs=pl.BlockSpec((group, rows, columns), lambda k: (k, 0, 0)),
        compiler_params=pltpu.CompilerParams(vmem_limit_bytes=40 * MIB),
        cost_estimate=LITTLE,
        name="near_product",
    )(blocks, slab)


def far_product(blocks, arrived, first, before, place, devices, per_tile):
    dirs, _, rows, wide = blocks.shape
    cap, _, _, boxes, columns = arrived[0].shape
    count = len(arrived)
    slots = count * cap
    last = place is not None
    group = STEP_DIRS if dirs % STEP_DIRS == 0 else 1

    def kernel(block_ref, before_ref, *refs):
        taken, outs = refs[:count], refs[count:]
        step = pl.program_id(0)
        for inner in range(group):
            sources = []
            for index in range(count):
                for slot in range(cap):
                    pieces = [taken[index][slot, piece, inner] for piece in range(per_tile)]
                    sources.append(stack_rows(jnp.concatenate(pieces, axis=0)))
            total = before_ref[inner] + jnp.dot(
                wide_block(block_ref.at[inner], slots),
                jnp.concatenate(sources, axis=0),
                preferred_element_type=jnp.float32,
            )
            if last:
                total_ref = outs[-1]
                total_ref[inner] = total
                for index in range(devices):
                    at = pl.multiple_of((outs[-2][0] ^ index) * boxes, boxes)
                    outs[index][step * group + inner] = total_ref[inner, pl.ds(at, boxes), :].astype(jnp.bfloat16)
            else:
                outs[0][inner] = total

    def kernel_last(place_ref, block_ref, before_ref, *refs):
        kernel(block_ref, before_ref, *refs[: count + devices], place_ref, refs[count + devices])

    in_specs = [
        pl.BlockSpec((group, slots, rows, wide), lambda k: (k, first, 0, 0)),
        pl.BlockSpec((group, rows, columns), lambda k: (k, 0, 0)),
    ] + [pl.BlockSpec((cap, per_tile, group, boxes, columns), lambda k: (0, 0, k, 0, 0))] * count
    operands = [blocks, before, *arrived]
    if last:
        in_specs = smem(1) + in_specs
        operands = [place] + operands
        out_shape = [jax.ShapeDtypeStruct((dirs, boxes, columns), jnp.bfloat16)] * devices
        out_specs = [pl.BlockSpec((dirs, boxes, columns), lambda k: (0, 0, 0))] * devices
        scratch = [pltpu.VMEM((group, rows, columns), jnp.float32)]
    else:
        out_shape = [jax.ShapeDtypeStruct((dirs, rows, columns), jnp.float32)]
        out_specs = [pl.BlockSpec((group, rows, columns), lambda k: (k, 0, 0))]
        scratch = []
    return pl.pallas_call(
        kernel_last if last else kernel,
        grid=(dirs // group,),
        out_shape=out_shape,
        in_specs=in_specs,
        out_specs=out_specs,
        scratch_shapes=scratch,
        compiler_params=pltpu.CompilerParams(vmem_limit_bytes=40 * MIB),
        cost_estimate=LITTLE,
        name="far_last" if last else "far_first",
    )(*operands)


def disaggregate(returned, disaggregation, place):
    dirs, boxes, columns = returned[0].shape
    devices = len(returned)
    unknowns = disaggregation.shape[0]
    all_dirs = disaggregation.shape[1] // 2
    step = boxes // 2

    def kernel(place_ref, dis_ref, *refs):
        out_ref, scratch = refs[devices], refs[devices + 1]
        for index, other in enumerate(order(devices)):
            first = (place_ref[0] ^ other) * dirs
            for inner in range(dirs):
                at = pl.multiple_of((first + inner) * step, step)
                scratch[pl.ds(at, step), :] = refs[index][inner].astype(jnp.float32)
        matrix = dis_ref[...]
        for box in range(step):
            rows = stack_rows(scratch[pl.ds(box, all_dirs, stride=step), :])
            out_ref[box] = jnp.dot(matrix, rows, preferred_element_type=jnp.float32).astype(jnp.bfloat16)

    return pl.pallas_call(
        kernel,
        grid=(boxes // step,),
        out_shape=jax.ShapeDtypeStruct((boxes, unknowns, columns), jnp.bfloat16),
        in_specs=smem(1)
        + [pl.BlockSpec(disaggregation.shape, lambda i: (0, 0))]
        + [pl.BlockSpec((dirs, step, columns), lambda i: (0, i, 0))] * devices,
        out_specs=pl.BlockSpec((step, unknowns, columns), lambda i: (i, 0, 0)),
        scratch_shapes=[pltpu.VMEM((all_dirs * step, columns), jnp.float32)],
        compiler_params=pltpu.CompilerParams(vmem_limit_bytes=20 * MIB),
        cost_estimate=LITTLE,
        name="disaggregate",
    )(place, disaggregation, *[returned[other] for other in order(devices)])


def crossed(pieces, axis):
    count = len(pieces)
    moved = [lax.ppermute(pieces[step], axis, [(i, i ^ step) for i in range(count)]) for step in range(1, count)]
    return [pieces[0]] + moved


def make_local(sectors, devices):
    partners = sectors - 1
    barrier = lax.optimization_barrier

    def local(
        fields,
        aggregation,
        operators,
        disaggregation,
        near_tile,
        near_operator,
        far_slot,
        far_operator,
        send_tiles,
    ):
        per_tile = operators.shape[2] // fields.shape[0]
        cap = send_tiles.shape[2]
        where = lax.axis_index("sector").astype(jnp.int32).reshape(1)
        place = lax.axis_index("dir").astype(jnp.int32).reshape(1)
        listing = lax.dynamic_index_in_dim(jnp.swapaxes(send_tiles, 1, 2), where[0], 0, keepdims=False)
        outgoing = list(aggregate(fields, aggregation, place, devices))
        outgoing[1], listing = barrier((outgoing[1], listing))
        pieces = crossed(outgoing, "dir")
        slab, leaving = pick(pieces, listing, where, place, partners, per_tile)
        leaving, tile_index = barrier((leaving, near_tile))
        ranks = sorted(range(1, sectors), key=lambda step: 2 - step if step <= 2 else step - 1)
        arrived = crossed([leaving[0], *leaving], "sector")[1:]
        arrived = [arrived[step - 1] for step in ranks]
        near_blocks, far_blocks = build(
            operators, tile_index, near_operator, far_slot, far_operator, where, partners, cap
        )
        total = near_product(near_blocks, slab, per_tile)
        total = far_product(far_blocks, arrived[:-1], 0, total, None, devices, per_tile)[0]
        incoming = far_product(far_blocks, arrived[-1:], partners - 1, total, place, devices, per_tile)
        returned = crossed(incoming, "dir")
        return disaggregate(returned, disaggregation, place)

    return local


def solution(mesh):
    placed = (
        P(("sector", "dir"), None, None),
        P(),
        P(None, "dir", None, None),
        P(),
        P("sector", None),
        P("sector", None),
        P("sector", None),
        P("sector", None),
        P(),
    )
    return jax.shard_map(
        make_local(mesh.shape["sector"], mesh.shape["dir"]),
        mesh=mesh,
        in_specs=placed,
        out_specs=P(("sector", "dir"), None, None),
        check_vma=False,
    )
```

```python
import jax
import jax.numpy as jnp
from jax import lax
from jax.experimental import pallas as pl
from jax.experimental.pallas import tpu as pltpu
from jax.sharding import PartitionSpec as P

MIB = 1024 * 1024
STEP_DIRS = 2
AGG_MIB = 20
OP_CUTS = 4
OUT_CUTS = 8
LITTLE = pl.CostEstimate(flops=1, bytes_accessed=1, transcendentals=0)


def order(count):
    return sorted(range(count), key=lambda step: (step == 0, -bin(step >> 1).count("1"), -(step & 1), step))


def turned(values):
    half = values.shape[-1] // 2
    lane = lax.broadcasted_iota(jnp.int32, values.shape, values.ndim - 1)
    moved = pltpu.roll(values, half, values.ndim - 1)
    return jnp.where(lane < half, -moved, moved)


def stack_rows(values):
    wide = values.astype(jnp.float32)
    return jnp.concatenate([wide, turned(wide)], axis=0).astype(jnp.bfloat16)


def vmem(count):
    return [pl.BlockSpec(memory_space=pltpu.VMEM)] * count


def smem(count):
    return [pl.BlockSpec(memory_space=pltpu.SMEM)] * count


def aggregate(fields, aggregation, place, devices):
    boxes, unknowns, columns = fields.shape
    all_dirs = aggregation.shape[0]
    part = all_dirs // devices

    def kernel(place_ref, fields_ref, agg_ref, *refs):
        outs, scratch = refs[:devices], refs[devices]
        matrix = jnp.concatenate([agg_ref[:, :unknowns], agg_ref[:, unknowns:]], axis=0)
        for box in range(boxes):
            both = jnp.dot(matrix, fields_ref[box], preferred_element_type=jnp.float32)
            scratch[pl.ds(box * (all_dirs + 1), all_dirs), :] = both[:all_dirs] + turned(both[all_dirs:])
        for step in range(devices):
            first = (place_ref[0] ^ step) * part
            for inner in range(part):
                rows = scratch[pl.ds(first + inner, boxes, stride=all_dirs + 1), :]
                outs[step][inner] = rows.astype(jnp.bfloat16)

    return pl.pallas_call(
        kernel,
        out_shape=[jax.ShapeDtypeStruct((part, boxes, columns), jnp.bfloat16)] * devices,
        in_specs=smem(1) + vmem(2),
        out_specs=vmem(devices),
        scratch_shapes=[pltpu.VMEM((boxes * (all_dirs + 1), columns), jnp.float32)],
        compiler_params=pltpu.CompilerParams(vmem_limit_bytes=AGG_MIB * MIB),
        cost_estimate=LITTLE,
        name="aggregate",
    )(place, fields, aggregation)


def pick(pieces, listing, where, place, partners, per_tile):
    devices = len(pieces)
    dirs, boxes, columns = pieces[0].shape
    cap = listing.shape[0]

    def kernel(listing_ref, where_ref, place_ref, *refs):
        slab_ref, outs = refs[devices], refs[devices + 1 :]
        for index, step in enumerate(order(devices)):
            slab_ref[place_ref[0] ^ step] = refs[index][...]
        for index in range(partners):
            other = where_ref[0] ^ (index + 1)
            for slot in range(cap):
                tile = listing_ref[slot, other]
                outs[index][slot] = slab_ref[pl.ds(tile * per_tile, per_tile)]

    shapes = [(devices, dirs, boxes, columns)] + [(cap, per_tile, dirs, boxes, columns)] * partners
    outs = pl.pallas_call(
        kernel,
        out_shape=[jax.ShapeDtypeStruct(shape, jnp.bfloat16) for shape in shapes],
        in_specs=smem(3) + vmem(devices),
        out_specs=vmem(len(shapes)),
        compiler_params=pltpu.CompilerParams(vmem_limit_bytes=20 * MIB),
        cost_estimate=LITTLE,
        name="pick",
    )(listing, where, place, *[pieces[step] for step in order(devices)])
    return outs[0], outs[1:]


def build(operators, near_tile, near_operator, far_slot, far_operator, where, partners, cap):
    count, dirs, rows, wide = operators.shape
    tiles, entries = near_tile.shape
    far_entries = far_slot.shape[1]
    slots = partners * cap
    group = min(4, tiles)
    total = entries + far_entries
    cuts = OP_CUTS if count % OP_CUTS == 0 else 1
    size = count // cuts
    tables = (near_tile, near_operator, far_slot, far_operator)

    def kernel(where_ref, *refs):
        sources, op_hbm, near_out, far_out, last_out = refs[:4], refs[4], refs[5], refs[6], refs[7]
        listed, slot_table, op_table, ops, table_sem, op_sem = refs[8:12], refs[12], refs[13], refs[14], refs[15], refs[16]
        sums = refs[17:]
        near_sum, far_sum = sums[:group], sums[group:]
        now = pl.program_id(0)

        def table_copy(index):
            return pltpu.make_async_copy(sources[index], listed[index], table_sem.at[index])

        def op_copy(direction, cut):
            at = pl.ds(cut * size, size)
            return pltpu.make_async_copy(op_hbm.at[at, direction], ops.at[direction, at], op_sem.at[direction, cut])

        @pl.when(now == 0)
        def _():
            for index in range(4):
                table_copy(index).start()
            for direction in range(dirs):
                for cut in range(cuts):
                    op_copy(direction, cut).start()
            for index in range(4):
                table_copy(index).wait()
            for tile in range(tiles):

                def fill(entry, _):
                    slot_table[tile * total + entry] = listed[0][tile, entry]
                    op_table[tile * total + entry] = listed[1][tile, entry]
                    return 0

                def fill_far(entry, _):
                    place = listed[2][tile, entry]
                    sector = lax.div(place, cap)
                    step = sector ^ where_ref[0]
                    slot = (jnp.where(step <= 2, 2 - step, step - 1)) * cap + place - sector * cap
                    slot_table[tile * total + entries + entry] = slot
                    op_table[tile * total + entries + entry] = listed[3][tile, entry]
                    return 0

                lax.fori_loop(0, entries, fill, 0, unroll=4)
                lax.fori_loop(0, far_entries, fill_far, 0, unroll=4)

        for cut in range(cuts):
            op_copy(now, cut).wait()
        for base in range(0, tiles, group):
            for ref in sums:
                ref[...] = jnp.zeros_like(ref)
            for entry in range(total):
                for t in range(group):
                    at = (base + t) * total + entry
                    kept = near_sum[t] if entry < entries else far_sum[t]
                    kept[slot_table[at]] += ops[now, op_table[at]].astype(jnp.float32)
            for t in range(group):
                at = pl.ds((base + t) * rows, rows)
                near_out[:, at, :] = near_sum[t][...].astype(jnp.bfloat16)
                far_out[:, at, :] = far_sum[t][: slots - cap].astype(jnp.bfloat16)
                last_out[:, at, :] = far_sum[t][slots - cap :].astype(jnp.bfloat16)

    need = 2 * operators.size + 4 * group * (tiles + slots) * rows * wide + 8 * (tiles + slots) * tiles * rows * wide
    return pl.pallas_call(
        kernel,
        grid=(dirs,),
        out_shape=[
            jax.ShapeDtypeStruct((dirs, tiles, tiles * rows, wide), jnp.bfloat16),
            jax.ShapeDtypeStruct((dirs, slots - cap, tiles * rows, wide), jnp.bfloat16),
            jax.ShapeDtypeStruct((dirs, cap, tiles * rows, wide), jnp.bfloat16),
        ],
        in_specs=smem(1) + [pl.BlockSpec(memory_space=pltpu.HBM)] * 5,
        out_specs=[
            pl.BlockSpec((None, tiles, tiles * rows, wide), lambda k: (k, 0, 0, 0)),
            pl.BlockSpec((None, slots - cap, tiles * rows, wide), lambda k: (k, 0, 0, 0)),
            pl.BlockSpec((None, cap, tiles * rows, wide), lambda k: (k, 0, 0, 0)),
        ],
        scratch_shapes=[pltpu.SMEM(table.shape, jnp.int32) for table in tables]
        + [pltpu.SMEM((tiles * total,), jnp.int32)] * 2
        + [
            pltpu.VMEM((dirs, count, rows, wide), jnp.bfloat16),
            pltpu.SemaphoreType.DMA((4,)),
            pltpu.SemaphoreType.DMA((dirs, cuts)),
        ]
        + [pltpu.VMEM((tiles, rows, wide), jnp.float32)] * group
        + [pltpu.VMEM((slots, rows, wide), jnp.float32)] * group,
        compiler_params=pltpu.CompilerParams(vmem_limit_bytes=need + 4 * MIB),
        cost_estimate=LITTLE,
        name="build",
    )(where, *tables, operators)


def wide_block(block_ref, slots):
    return jnp.concatenate([block_ref[slot] for slot in range(slots)], axis=1)


def near_product(blocks, slab, per_tile):
    dirs, tiles, rows, wide = blocks.shape
    devices, _, boxes, columns = slab.shape
    group = STEP_DIRS if dirs % STEP_DIRS == 0 else 1

    def kernel(block_ref, slab_ref, out_ref):
        for inner in range(group):
            sources = []
            for tile in range(tiles):
                pieces = [slab_ref[tile * per_tile + piece, inner] for piece in range(per_tile)]
                sources.append(stack_rows(jnp.concatenate(pieces, axis=0)))
            out_ref[inner] = jnp.dot(
                wide_block(block_ref.at[inner], tiles),
                jnp.concatenate(sources, axis=0),
                preferred_element_type=jnp.float32,
            )

    return pl.pallas_call(
        kernel,
        grid=(dirs // group,),
        out_shape=jax.ShapeDtypeStruct((dirs, rows, columns), jnp.float32),
        in_specs=[
            pl.BlockSpec((group, tiles, rows, wide), lambda k: (k, 0, 0, 0)),
            pl.BlockSpec((devices, group, boxes, columns), lambda k: (0, k, 0, 0)),
        ],
        out_specs=pl.BlockSpec((group, rows, columns), lambda k: (k, 0, 0)),
        compiler_params=pltpu.CompilerParams(vmem_limit_bytes=40 * MIB),
        cost_estimate=LITTLE,
        name="near_product",
    )(blocks, slab)


def far_sources(arrived, inner):
    sources = []
    for piece_ref in arrived:
        for slot in range(piece_ref.shape[0]):
            pieces = [piece_ref[slot, piece, inner] for piece in range(piece_ref.shape[1])]
            sources.append(stack_rows(jnp.concatenate(pieces, axis=0)))
    return jnp.concatenate(sources, axis=0)


def far_first(blocks, arrived, before):
    dirs, slots, rows, wide = blocks.shape
    cap, per_tile, _, boxes, columns = arrived[0].shape
    count = len(arrived)
    group = STEP_DIRS if dirs % STEP_DIRS == 0 else 1

    def kernel(block_ref, before_ref, *refs):
        for inner in range(group):
            refs[count][inner] = before_ref[inner] + jnp.dot(
                wide_block(block_ref.at[inner], slots),
                far_sources(refs[:count], inner),
                preferred_element_type=jnp.float32,
            )

    return pl.pallas_call(
        kernel,
        grid=(dirs // group,),
        out_shape=jax.ShapeDtypeStruct((dirs, rows, columns), jnp.float32),
        in_specs=[
            pl.BlockSpec((group, slots, rows, wide), lambda k: (k, 0, 0, 0)),
            pl.BlockSpec((group, rows, columns), lambda k: (k, 0, 0)),
        ]
        + [pl.BlockSpec((cap, per_tile, group, boxes, columns), lambda k: (0, 0, k, 0, 0))] * count,
        out_specs=pl.BlockSpec((group, rows, columns), lambda k: (k, 0, 0)),
        compiler_params=pltpu.CompilerParams(vmem_limit_bytes=40 * MIB),
        cost_estimate=LITTLE,
        name="far_first",
    )(blocks, before, *arrived)


def far_last(blocks, arrived, before, place, devices):
    dirs, slots, rows, wide = blocks.shape
    boxes, columns = arrived.shape[-2:]

    def kernel(place_ref, block_ref, before_ref, arrived_ref, *refs):
        outs, total_ref = refs[:devices], refs[devices]
        for inner in range(dirs):
            total_ref[inner] = before_ref[inner] + jnp.dot(
                wide_block(block_ref.at[inner], slots),
                far_sources([arrived_ref], inner),
                preferred_element_type=jnp.float32,
            )
        for index in range(devices):
            at = pl.multiple_of((place_ref[0] ^ index) * boxes, boxes)
            for inner in range(dirs):
                outs[index][inner] = total_ref[inner, pl.ds(at, boxes), :].astype(jnp.bfloat16)

    return pl.pallas_call(
        kernel,
        out_shape=[jax.ShapeDtypeStruct((dirs, boxes, columns), jnp.bfloat16)] * devices,
        in_specs=smem(1) + vmem(3),
        out_specs=vmem(devices),
        scratch_shapes=[pltpu.VMEM((dirs, rows, columns), jnp.float32)],
        compiler_params=pltpu.CompilerParams(vmem_limit_bytes=20 * MIB),
        cost_estimate=LITTLE,
        name="far_last",
    )(place, blocks, before, arrived)


def disaggregate(returned, disaggregation, place):
    dirs, boxes, columns = returned[0].shape
    devices = len(returned)
    unknowns = disaggregation.shape[0]
    all_dirs = disaggregation.shape[1] // 2
    cuts = OUT_CUTS if boxes % OUT_CUTS == 0 else 1
    size = boxes // cuts

    def kernel(place_ref, dis_ref, *refs):
        out_hbm, scratch, result, sem = refs[devices:]
        for index, other in enumerate(order(devices)):
            first = (place_ref[0] ^ other) * dirs
            for inner in range(dirs):
                at = (first + inner) * (boxes + 1)
                scratch[pl.ds(at, boxes), :] = refs[index][inner].astype(jnp.float32)
        matrix = dis_ref[...]
        copies = []
        for cut in range(cuts):
            for box in range(cut * size, (cut + 1) * size):
                rows = stack_rows(scratch[pl.ds(box, all_dirs, stride=boxes + 1), :])
                result[box] = jnp.dot(matrix, rows, preferred_element_type=jnp.float32).astype(jnp.bfloat16)
            at = pl.ds(cut * size, size)
            copies.append(pltpu.make_async_copy(result.at[at], out_hbm.at[at], sem.at[cut]))
            copies[cut].start()
        for copy in copies:
            copy.wait()

    return pl.pallas_call(
        kernel,
        out_shape=jax.ShapeDtypeStruct((boxes, unknowns, columns), jnp.bfloat16),
        in_specs=smem(1) + vmem(1 + devices),
        out_specs=pl.BlockSpec(memory_space=pl.ANY),
        scratch_shapes=[
            pltpu.VMEM((all_dirs * (boxes + 1), columns), jnp.float32),
            pltpu.VMEM((boxes, unknowns, columns), jnp.bfloat16),
            pltpu.SemaphoreType.DMA((cuts,)),
        ],
        compiler_params=pltpu.CompilerParams(vmem_limit_bytes=20 * MIB),
        cost_estimate=LITTLE,
        name="disaggregate",
    )(place, disaggregation, *[returned[other] for other in order(devices)])


def crossed(pieces, axis):
    count = len(pieces)
    moved = [lax.ppermute(pieces[step], axis, [(i, i ^ step) for i in range(count)]) for step in range(1, count)]
    return [pieces[0]] + moved


def make_local(sectors, devices):
    partners = sectors - 1
    barrier = lax.optimization_barrier

    def local(
        fields,
        aggregation,
        operators,
        disaggregation,
        near_tile,
        near_operator,
        far_slot,
        far_operator,
        send_tiles,
    ):
        per_tile = operators.shape[2] // fields.shape[0]
        cap = send_tiles.shape[2]
        where = lax.axis_index("sector").astype(jnp.int32).reshape(1)
        place = lax.axis_index("dir").astype(jnp.int32).reshape(1)
        listing = lax.dynamic_index_in_dim(jnp.swapaxes(send_tiles, 1, 2), where[0], 0, keepdims=False)
        outgoing = list(aggregate(fields, aggregation, place, devices))
        outgoing[1], listing = barrier((outgoing[1], listing))
        pieces = crossed(outgoing, "dir")
        slab, leaving = pick(pieces, listing, where, place, partners, per_tile)
        leaving, tile_index = barrier((leaving, near_tile))
        ranks = sorted(range(1, sectors), key=lambda step: 2 - step if step <= 2 else step - 1)
        arrived = crossed([leaving[0], *leaving], "sector")[1:]
        arrived = [arrived[step - 1] for step in ranks]
        near_blocks, far_blocks, last_blocks = build(
            operators, tile_index, near_operator, far_slot, far_operator, where, partners, cap
        )
        total = near_product(near_blocks, slab, per_tile)
        total = far_first(far_blocks, arrived[:-1], total)
        incoming = far_last(last_blocks, arrived[-1], total, place, devices)
        returned = crossed(incoming, "dir")
        return disaggregate(returned, disaggregation, place)

    return local


def solution(mesh):
    placed = (
        P(("sector", "dir"), None, None),
        P(),
        P(None, "dir", None, None),
        P(),
        P("sector", None),
        P("sector", None),
        P("sector", None),
        P("sector", None),
        P(),
    )
    return jax.shard_map(
        make_local(mesh.shape["sector"], mesh.shape["dir"]),
        mesh=mesh,
        in_specs=placed,
        out_specs=P(("sector", "dir"), None, None),
        check_vma=False,
    )
```

```python
import jax
import jax.numpy as jnp
from jax import lax
from jax.experimental import pallas as pl
from jax.experimental.pallas import tpu as pltpu
from jax.sharding import PartitionSpec as P

MIB = 1024 * 1024
STEP_DIRS = 2
AGG_MIB = 20
OP_CUTS = 4
OUT_CUTS = 8
LITTLE = pl.CostEstimate(flops=1, bytes_accessed=1, transcendentals=0)


def order(count):
    return sorted(range(count), key=lambda step: (step == 0, -bin(step >> 1).count("1"), -(step & 1), step))


def turned(values):
    half = values.shape[-1] // 2
    lane = lax.broadcasted_iota(jnp.int32, values.shape, values.ndim - 1)
    moved = pltpu.roll(values, half, values.ndim - 1)
    return jnp.where(lane < half, -moved, moved)


def stack_rows(values):
    wide = values.astype(jnp.float32)
    return jnp.concatenate([wide, turned(wide)], axis=0).astype(jnp.bfloat16)


def vmem(count):
    return [pl.BlockSpec(memory_space=pltpu.VMEM)] * count


def smem(count):
    return [pl.BlockSpec(memory_space=pltpu.SMEM)] * count


def aggregate(fields, aggregation, place, devices):
    boxes, unknowns, columns = fields.shape
    all_dirs = aggregation.shape[0]
    part = all_dirs // devices

    def kernel(place_ref, fields_ref, agg_ref, *refs):
        outs, scratch = refs[:devices], refs[devices]
        matrix = jnp.concatenate([agg_ref[:, :unknowns], agg_ref[:, unknowns:]], axis=0)
        for box in range(boxes):
            both = jnp.dot(matrix, fields_ref[box], preferred_element_type=jnp.float32)
            scratch[pl.ds(box * (all_dirs + 1), all_dirs), :] = both[:all_dirs] + turned(both[all_dirs:])
        for step in range(devices):
            first = (place_ref[0] ^ step) * part
            for inner in range(part):
                rows = scratch[pl.ds(first + inner, boxes, stride=all_dirs + 1), :]
                outs[step][inner] = rows.astype(jnp.bfloat16)

    return pl.pallas_call(
        kernel,
        out_shape=[jax.ShapeDtypeStruct((part, boxes, columns), jnp.bfloat16)] * devices,
        in_specs=smem(1) + vmem(2),
        out_specs=vmem(devices),
        scratch_shapes=[pltpu.VMEM((boxes * (all_dirs + 1), columns), jnp.float32)],
        compiler_params=pltpu.CompilerParams(vmem_limit_bytes=AGG_MIB * MIB),
        cost_estimate=LITTLE,
        name="aggregate",
    )(place, fields, aggregation)


def pick(pieces, listing, where, place, partners, per_tile):
    devices = len(pieces)
    dirs, boxes, columns = pieces[0].shape
    cap = listing.shape[0]

    def kernel(listing_ref, where_ref, place_ref, *refs):
        slab_ref, outs = refs[devices], refs[devices + 1 :]
        for index, step in enumerate(order(devices)):
            slab_ref[place_ref[0] ^ step] = refs[index][...]
        for index in range(partners):
            other = where_ref[0] ^ (index + 1)
            for slot in range(cap):
                tile = listing_ref[slot, other]
                outs[index][slot] = slab_ref[pl.ds(tile * per_tile, per_tile)]

    shapes = [(devices, dirs, boxes, columns)] + [(cap, per_tile, dirs, boxes, columns)] * partners
    outs = pl.pallas_call(
        kernel,
        out_shape=[jax.ShapeDtypeStruct(shape, jnp.bfloat16) for shape in shapes],
        in_specs=smem(3) + vmem(devices),
        out_specs=vmem(len(shapes)),
        compiler_params=pltpu.CompilerParams(vmem_limit_bytes=20 * MIB),
        cost_estimate=LITTLE,
        name="pick",
    )(listing, where, place, *[pieces[step] for step in order(devices)])
    return outs[0], outs[1:]


def build(operators, near_tile, near_operator, far_slot, far_operator, where, partners, cap):
    count, dirs, rows, wide = operators.shape
    tiles, entries = near_tile.shape
    far_entries = far_slot.shape[1]
    slots = partners * cap
    group = min(4, tiles)
    total = entries + far_entries
    cuts = OP_CUTS if count % OP_CUTS == 0 else 1
    size = count // cuts
    tables = (near_tile, near_operator, far_slot, far_operator)

    def kernel(where_ref, *refs):
        sources, op_hbm, near_out, far_out, last_out = refs[:4], refs[4], refs[5], refs[6], refs[7]
        listed, slot_table, op_table, ops, table_sem, op_sem = refs[8:12], refs[12], refs[13], refs[14], refs[15], refs[16]
        sums = refs[17:]
        near_sum, far_sum = sums[:group], sums[group:]
        now = pl.program_id(0)

        def table_copy(index):
            return pltpu.make_async_copy(sources[index], listed[index], table_sem.at[index])

        def op_copy(direction, cut):
            at = pl.ds(cut * size, size)
            return pltpu.make_async_copy(op_hbm.at[at, direction], ops.at[direction, at], op_sem.at[direction, cut])

        @pl.when(now == 0)
        def _():
            for index in range(4):
                table_copy(index).start()
            for direction in range(dirs):
                for cut in range(cuts):
                    op_copy(direction, cut).start()
            for index in range(4):
                table_copy(index).wait()
            for tile in range(tiles):

                def fill(entry, _):
                    slot_table[tile * total + entry] = listed[0][tile, entry]
                    op_table[tile * total + entry] = listed[1][tile, entry]
                    return 0

                def fill_far(entry, _):
                    place = listed[2][tile, entry]
                    sector = lax.div(place, cap)
                    step = sector ^ where_ref[0]
                    slot = (jnp.where(step <= 2, 2 - step, step - 1)) * cap + place - sector * cap
                    slot_table[tile * total + entries + entry] = slot
                    op_table[tile * total + entries + entry] = listed[3][tile, entry]
                    return 0

                lax.fori_loop(0, entries, fill, 0, unroll=4)
                lax.fori_loop(0, far_entries, fill_far, 0, unroll=4)

        for cut in range(cuts):
            op_copy(now, cut).wait()
        for base in range(0, tiles, group):
            for ref in sums:
                ref[...] = jnp.zeros_like(ref)
            for entry in range(total):
                for t in range(group):
                    at = (base + t) * total + entry
                    kept = near_sum[t] if entry < entries else far_sum[t]
                    kept[slot_table[at]] += ops[now, op_table[at]].astype(jnp.float32)
            for t in range(group):
                at = pl.ds((base + t) * rows, rows)
                near_out[:, at, :] = near_sum[t][...].astype(jnp.bfloat16)
                far_out[:, at, :] = far_sum[t][: slots - cap].astype(jnp.bfloat16)
                last_out[:, at, :] = far_sum[t][slots - cap :].astype(jnp.bfloat16)

    need = 2 * operators.size + 4 * group * (tiles + slots) * rows * wide + 8 * (tiles + slots) * tiles * rows * wide
    return pl.pallas_call(
        kernel,
        grid=(dirs,),
        out_shape=[
            jax.ShapeDtypeStruct((dirs, tiles, tiles * rows, wide), jnp.bfloat16),
            jax.ShapeDtypeStruct((dirs, slots - cap, tiles * rows, wide), jnp.bfloat16),
            jax.ShapeDtypeStruct((dirs, cap, tiles * rows, wide), jnp.bfloat16),
        ],
        in_specs=smem(1) + [pl.BlockSpec(memory_space=pltpu.HBM)] * 5,
        out_specs=[
            pl.BlockSpec((None, tiles, tiles * rows, wide), lambda k: (k, 0, 0, 0)),
            pl.BlockSpec((None, slots - cap, tiles * rows, wide), lambda k: (k, 0, 0, 0)),
            pl.BlockSpec((None, cap, tiles * rows, wide), lambda k: (k, 0, 0, 0)),
        ],
        scratch_shapes=[pltpu.SMEM(table.shape, jnp.int32) for table in tables]
        + [pltpu.SMEM((tiles * total,), jnp.int32)] * 2
        + [
            pltpu.VMEM((dirs, count, rows, wide), jnp.bfloat16),
            pltpu.SemaphoreType.DMA((4,)),
            pltpu.SemaphoreType.DMA((dirs, cuts)),
        ]
        + [pltpu.VMEM((tiles, rows, wide), jnp.float32)] * group
        + [pltpu.VMEM((slots, rows, wide), jnp.float32)] * group,
        compiler_params=pltpu.CompilerParams(vmem_limit_bytes=need + 4 * MIB),
        cost_estimate=LITTLE,
        name="build",
    )(where, *tables, operators)


def wide_block(block_ref, slots):
    return jnp.concatenate([block_ref[slot] for slot in range(slots)], axis=1)


def near_product(blocks, slab, per_tile):
    dirs, tiles, rows, wide = blocks.shape
    devices, _, boxes, columns = slab.shape
    group = STEP_DIRS if dirs % STEP_DIRS == 0 else 1

    def kernel(block_ref, slab_ref, out_ref):
        for inner in range(group):
            sources = []
            for tile in range(tiles):
                pieces = [slab_ref[tile * per_tile + piece, inner] for piece in range(per_tile)]
                sources.append(stack_rows(jnp.concatenate(pieces, axis=0)))
            out_ref[inner] = jnp.dot(
                wide_block(block_ref.at[inner], tiles),
                jnp.concatenate(sources, axis=0),
                preferred_element_type=jnp.float32,
            )

    return pl.pallas_call(
        kernel,
        grid=(dirs // group,),
        out_shape=jax.ShapeDtypeStruct((dirs, rows, columns), jnp.float32),
        in_specs=[
            pl.BlockSpec((group, tiles, rows, wide), lambda k: (k, 0, 0, 0)),
            pl.BlockSpec((devices, group, boxes, columns), lambda k: (0, k, 0, 0)),
        ],
        out_specs=pl.BlockSpec((group, rows, columns), lambda k: (k, 0, 0)),
        compiler_params=pltpu.CompilerParams(vmem_limit_bytes=40 * MIB),
        cost_estimate=LITTLE,
        name="near_product",
    )(blocks, slab)


def far_sources(arrived, inner):
    sources = []
    for piece_ref in arrived:
        for slot in range(piece_ref.shape[0]):
            pieces = [piece_ref[slot, piece, inner] for piece in range(piece_ref.shape[1])]
            sources.append(stack_rows(jnp.concatenate(pieces, axis=0)))
    return jnp.concatenate(sources, axis=0)


def far_first(blocks, arrived, before):
    dirs, slots, rows, wide = blocks.shape
    cap, per_tile, _, boxes, columns = arrived[0].shape
    count = len(arrived)
    group = STEP_DIRS if dirs % STEP_DIRS == 0 else 1

    def kernel(block_ref, before_ref, *refs):
        for inner in range(group):
            refs[count][inner] = before_ref[inner] + jnp.dot(
                wide_block(block_ref.at[inner], slots),
                far_sources(refs[:count], inner),
                preferred_element_type=jnp.float32,
            )

    return pl.pallas_call(
        kernel,
        grid=(dirs // group,),
        out_shape=jax.ShapeDtypeStruct((dirs, rows, columns), jnp.float32),
        in_specs=[
            pl.BlockSpec((group, slots, rows, wide), lambda k: (k, 0, 0, 0)),
            pl.BlockSpec((group, rows, columns), lambda k: (k, 0, 0)),
        ]
        + [pl.BlockSpec((cap, per_tile, group, boxes, columns), lambda k: (0, 0, k, 0, 0))] * count,
        out_specs=pl.BlockSpec((group, rows, columns), lambda k: (k, 0, 0)),
        compiler_params=pltpu.CompilerParams(vmem_limit_bytes=40 * MIB),
        cost_estimate=LITTLE,
        name="far_first",
    )(blocks, before, *arrived)


def far_last(blocks, arrived, before, place, devices):
    dirs, slots, rows, wide = blocks.shape
    boxes, columns = arrived.shape[-2:]

    def kernel(place_ref, block_ref, before_ref, arrived_ref, *refs):
        outs, total_ref = refs[:devices], refs[devices]
        for inner in range(dirs):
            total_ref[inner] = before_ref[inner] + jnp.dot(
                wide_block(block_ref.at[inner], slots),
                far_sources([arrived_ref], inner),
                preferred_element_type=jnp.float32,
            )
        for index in range(devices):
            at = pl.multiple_of((place_ref[0] ^ index) * boxes, boxes)
            for inner in range(dirs):
                outs[index][inner] = total_ref[inner, pl.ds(at, boxes), :].astype(jnp.bfloat16)

    return pl.pallas_call(
        kernel,
        out_shape=[jax.ShapeDtypeStruct((dirs, boxes, columns), jnp.bfloat16)] * devices,
        in_specs=smem(1) + vmem(3),
        out_specs=vmem(devices),
        scratch_shapes=[pltpu.VMEM((dirs, rows, columns), jnp.float32)],
        compiler_params=pltpu.CompilerParams(vmem_limit_bytes=20 * MIB),
        cost_estimate=LITTLE,
        name="far_last",
    )(place, blocks, before, arrived)


def disaggregate(returned, disaggregation, place):
    dirs, boxes, columns = returned[0].shape
    devices = len(returned)
    unknowns = disaggregation.shape[0]
    all_dirs = disaggregation.shape[1] // 2
    cuts = OUT_CUTS if boxes % OUT_CUTS == 0 else 1
    size = boxes // cuts

    def kernel(place_ref, dis_ref, *refs):
        out_hbm, scratch, result, sem = refs[devices:]
        for index, other in enumerate(order(devices)):
            first = (place_ref[0] ^ other) * dirs
            for inner in range(dirs):
                at = (first + inner) * (boxes + 1)
                scratch[pl.ds(at, boxes), :] = refs[index][inner].astype(jnp.float32)
        matrix = dis_ref[...]
        copies = []
        for cut in range(cuts):
            for box in range(cut * size, (cut + 1) * size):
                rows = stack_rows(scratch[pl.ds(box, all_dirs, stride=boxes + 1), :])
                result[box] = jnp.dot(matrix, rows, preferred_element_type=jnp.float32).astype(jnp.bfloat16)
            at = pl.ds(cut * size, size)
            copies.append(pltpu.make_async_copy(result.at[at], out_hbm.at[at], sem.at[cut]))
            copies[cut].start()
        for copy in copies:
            copy.wait()

    return pl.pallas_call(
        kernel,
        out_shape=jax.ShapeDtypeStruct((boxes, unknowns, columns), jnp.bfloat16),
        in_specs=smem(1) + vmem(1 + devices),
        out_specs=pl.BlockSpec(memory_space=pl.ANY),
        scratch_shapes=[
            pltpu.VMEM((all_dirs * (boxes + 1), columns), jnp.float32),
            pltpu.VMEM((boxes, unknowns, columns), jnp.bfloat16),
            pltpu.SemaphoreType.DMA((cuts,)),
        ],
        compiler_params=pltpu.CompilerParams(vmem_limit_bytes=20 * MIB),
        cost_estimate=LITTLE,
        name="disaggregate",
    )(place, disaggregation, *[returned[other] for other in order(devices)])


def crossed(pieces, axis):
    count = len(pieces)
    moved = [lax.ppermute(pieces[step], axis, [(i, i ^ step) for i in range(count)]) for step in range(1, count)]
    return [pieces[0]] + moved


def make_local(sectors, devices):
    partners = sectors - 1
    barrier = lax.optimization_barrier

    def local(
        fields,
        aggregation,
        operators,
        disaggregation,
        near_tile,
        near_operator,
        far_slot,
        far_operator,
        send_tiles,
    ):
        per_tile = operators.shape[2] // fields.shape[0]
        cap = send_tiles.shape[2]
        where = lax.axis_index("sector").astype(jnp.int32).reshape(1)
        place = lax.axis_index("dir").astype(jnp.int32).reshape(1)
        listing = lax.dynamic_index_in_dim(jnp.swapaxes(send_tiles, 1, 2), where[0], 0, keepdims=False)
        outgoing = list(aggregate(fields, aggregation, place, devices))
        outgoing[0], listing = barrier((outgoing[0], listing))
        pieces = crossed(outgoing, "dir")
        slab, leaving = pick(pieces, listing, where, place, partners, per_tile)
        leaving, tile_index = barrier((leaving, near_tile))
        ranks = sorted(range(1, sectors), key=lambda step: 2 - step if step <= 2 else step - 1)
        arrived = crossed([leaving[0], *leaving], "sector")[1:]
        arrived = [arrived[step - 1] for step in ranks]
        near_blocks, far_blocks, last_blocks = build(
            operators, tile_index, near_operator, far_slot, far_operator, where, partners, cap
        )
        total = near_product(near_blocks, slab, per_tile)
        total = far_first(far_blocks, arrived[:-1], total)
        incoming = far_last(last_blocks, arrived[-1], total, place, devices)
        returned = crossed(incoming, "dir")
        return disaggregate(returned, disaggregation, place)

    return local


def solution(mesh):
    placed = (
        P(("sector", "dir"), None, None),
        P(),
        P(None, "dir", None, None),
        P(),
        P("sector", None),
        P("sector", None),
        P("sector", None),
        P("sector", None),
        P(),
    )
    return jax.shard_map(
        make_local(mesh.shape["sector"], mesh.shape["dir"]),
        mesh=mesh,
        in_specs=placed,
        out_specs=P(("sector", "dir"), None, None),
        check_vma=False,
    )
```

```python
import jax
import jax.numpy as jnp
from jax import lax
from jax.experimental import pallas as pl
from jax.experimental.pallas import tpu as pltpu
from jax.sharding import PartitionSpec as P

MIB = 1024 * 1024
STEP_DIRS = 2
AGG_MIB = 20
OP_CUTS = 4
OUT_CUTS = 8
LITTLE = pl.CostEstimate(flops=1, bytes_accessed=1, transcendentals=0)


def order(count):
    return sorted(range(count), key=lambda step: (step == 0, -bin(step >> 1).count("1"), -(step & 1), step))


def turned(values):
    half = values.shape[-1] // 2
    lane = lax.broadcasted_iota(jnp.int32, values.shape, values.ndim - 1)
    moved = pltpu.roll(values, half, values.ndim - 1)
    return jnp.where(lane < half, -moved, moved)


def stack_rows(values):
    wide = values.astype(jnp.float32)
    return jnp.concatenate([wide, turned(wide)], axis=0).astype(jnp.bfloat16)


def vmem(count):
    return [pl.BlockSpec(memory_space=pltpu.VMEM)] * count


def smem(count):
    return [pl.BlockSpec(memory_space=pltpu.SMEM)] * count


def aggregate(fields, aggregation, place, devices):
    boxes, unknowns, columns = fields.shape
    all_dirs = aggregation.shape[0]
    part = all_dirs // devices

    def kernel(place_ref, fields_ref, agg_ref, *refs):
        outs, scratch = refs[:devices], refs[devices]
        matrix = jnp.concatenate([agg_ref[:, :unknowns], agg_ref[:, unknowns:]], axis=0)
        for box in range(boxes):
            both = jnp.dot(matrix, fields_ref[box], preferred_element_type=jnp.float32)
            scratch[pl.ds(box * (all_dirs + 1), all_dirs), :] = both[:all_dirs] + turned(both[all_dirs:])
        for step in range(devices):
            first = (place_ref[0] ^ step) * part
            for inner in range(part):
                rows = scratch[pl.ds(first + inner, boxes, stride=all_dirs + 1), :]
                outs[step][inner] = rows.astype(jnp.bfloat16)

    return pl.pallas_call(
        kernel,
        out_shape=[jax.ShapeDtypeStruct((part, boxes, columns), jnp.bfloat16)] * devices,
        in_specs=smem(1) + vmem(2),
        out_specs=vmem(devices),
        scratch_shapes=[pltpu.VMEM(((boxes + 1) * (all_dirs + 1), columns), jnp.float32)],
        compiler_params=pltpu.CompilerParams(vmem_limit_bytes=AGG_MIB * MIB),
        cost_estimate=LITTLE,
        name="aggregate",
    )(place, fields, aggregation)


def pick(pieces, listing, where, place, partners, per_tile):
    devices = len(pieces)
    dirs, boxes, columns = pieces[0].shape
    cap = listing.shape[0]

    def kernel(listing_ref, where_ref, place_ref, *refs):
        slab_ref, outs = refs[devices], refs[devices + 1 :]
        for index, step in enumerate(order(devices)):
            slab_ref[place_ref[0] ^ step] = refs[index][...]
        for index in range(partners):
            other = where_ref[0] ^ (index + 1)
            for slot in range(cap):
                tile = listing_ref[slot, other]
                outs[index][slot] = slab_ref[pl.ds(tile * per_tile, per_tile)]

    shapes = [(devices, dirs, boxes, columns)] + [(cap, per_tile, dirs, boxes, columns)] * partners
    outs = pl.pallas_call(
        kernel,
        out_shape=[jax.ShapeDtypeStruct(shape, jnp.bfloat16) for shape in shapes],
        in_specs=smem(3) + vmem(devices),
        out_specs=vmem(len(shapes)),
        compiler_params=pltpu.CompilerParams(vmem_limit_bytes=20 * MIB),
        cost_estimate=LITTLE,
        name="pick",
    )(listing, where, place, *[pieces[step] for step in order(devices)])
    return outs[0], outs[1:]


def build(operators, near_tile, near_operator, far_slot, far_operator, where, partners, cap):
    count, dirs, rows, wide = operators.shape
    tiles, entries = near_tile.shape
    far_entries = far_slot.shape[1]
    slots = partners * cap
    group = min(4, tiles)
    total = entries + far_entries
    cuts = OP_CUTS if count % OP_CUTS == 0 else 1
    size = count // cuts
    tables = (near_tile, near_operator, far_slot, far_operator)

    def kernel(where_ref, *refs):
        sources, op_hbm, near_out, far_out, last_out = refs[:4], refs[4], refs[5], refs[6], refs[7]
        listed, slot_table, op_table, ops, table_sem, op_sem = refs[8:12], refs[12], refs[13], refs[14], refs[15], refs[16]
        sums = refs[17:]
        near_sum, far_sum = sums[:group], sums[group:]
        now = pl.program_id(0)

        def table_copy(index):
            return pltpu.make_async_copy(sources[index], listed[index], table_sem.at[index])

        def op_copy(direction, cut):
            at = pl.ds(cut * size, size)
            return pltpu.make_async_copy(op_hbm.at[at, direction], ops.at[direction, at], op_sem.at[direction, cut])

        @pl.when(now == 0)
        def _():
            for index in range(4):
                table_copy(index).start()
            for direction in range(dirs):
                for cut in range(cuts):
                    op_copy(direction, cut).start()
            for index in range(4):
                table_copy(index).wait()
            for tile in range(tiles):

                def fill(entry, _):
                    slot_table[tile * total + entry] = listed[0][tile, entry]
                    op_table[tile * total + entry] = listed[1][tile, entry]
                    return 0

                def fill_far(entry, _):
                    place = listed[2][tile, entry]
                    sector = lax.div(place, cap)
                    step = sector ^ where_ref[0]
                    slot = (jnp.where(step <= 2, 2 - step, step - 1)) * cap + place - sector * cap
                    slot_table[tile * total + entries + entry] = slot
                    op_table[tile * total + entries + entry] = listed[3][tile, entry]
                    return 0

                lax.fori_loop(0, entries, fill, 0, unroll=4)
                lax.fori_loop(0, far_entries, fill_far, 0, unroll=4)

        for cut in range(cuts):
            op_copy(now, cut).wait()
        for base in range(0, tiles, group):
            for ref in sums:
                ref[...] = jnp.zeros_like(ref)
            for entry in range(total):
                for t in range(group):
                    at = (base + t) * total + entry
                    kept = near_sum[t] if entry < entries else far_sum[t]
                    kept[slot_table[at]] += ops[now, op_table[at]].astype(jnp.float32)
            for t in range(group):
                at = pl.ds((base + t) * rows, rows)
                near_out[:, at, :] = near_sum[t][...].astype(jnp.bfloat16)
                far_out[:, at, :] = far_sum[t][: slots - cap].astype(jnp.bfloat16)
                last_out[:, at, :] = far_sum[t][slots - cap :].astype(jnp.bfloat16)

    need = 2 * operators.size + 4 * group * (tiles + slots) * rows * wide + 8 * (tiles + slots) * tiles * rows * wide
    return pl.pallas_call(
        kernel,
        grid=(dirs,),
        out_shape=[
            jax.ShapeDtypeStruct((dirs, tiles, tiles * rows, wide), jnp.bfloat16),
            jax.ShapeDtypeStruct((dirs, slots - cap, tiles * rows, wide), jnp.bfloat16),
            jax.ShapeDtypeStruct((dirs, cap, tiles * rows, wide), jnp.bfloat16),
        ],
        in_specs=smem(1) + [pl.BlockSpec(memory_space=pltpu.HBM)] * 5,
        out_specs=[
            pl.BlockSpec((None, tiles, tiles * rows, wide), lambda k: (k, 0, 0, 0)),
            pl.BlockSpec((None, slots - cap, tiles * rows, wide), lambda k: (k, 0, 0, 0)),
            pl.BlockSpec((None, cap, tiles * rows, wide), lambda k: (k, 0, 0, 0)),
        ],
        scratch_shapes=[pltpu.SMEM(table.shape, jnp.int32) for table in tables]
        + [pltpu.SMEM((tiles * total,), jnp.int32)] * 2
        + [
            pltpu.VMEM((dirs, count, rows, wide), jnp.bfloat16),
            pltpu.SemaphoreType.DMA((4,)),
            pltpu.SemaphoreType.DMA((dirs, cuts)),
        ]
        + [pltpu.VMEM((tiles, rows, wide), jnp.float32)] * group
        + [pltpu.VMEM((slots, rows, wide), jnp.float32)] * group,
        compiler_params=pltpu.CompilerParams(vmem_limit_bytes=need + 4 * MIB),
        cost_estimate=LITTLE,
        name="build",
    )(where, *tables, operators)


def wide_block(block_ref, slots):
    return jnp.concatenate([block_ref[slot] for slot in range(slots)], axis=1)


def near_product(blocks, slab, per_tile):
    dirs, tiles, rows, wide = blocks.shape
    devices, _, boxes, columns = slab.shape
    group = STEP_DIRS if dirs % STEP_DIRS == 0 else 1

    def kernel(block_ref, slab_ref, out_ref):
        for inner in range(group):
            sources = []
            for tile in range(tiles):
                pieces = [slab_ref[tile * per_tile + piece, inner] for piece in range(per_tile)]
                sources.append(stack_rows(jnp.concatenate(pieces, axis=0)))
            out_ref[inner] = jnp.dot(
                wide_block(block_ref.at[inner], tiles),
                jnp.concatenate(sources, axis=0),
                preferred_element_type=jnp.float32,
            )

    return pl.pallas_call(
        kernel,
        grid=(dirs // group,),
        out_shape=jax.ShapeDtypeStruct((dirs, rows, columns), jnp.float32),
        in_specs=[
            pl.BlockSpec((group, tiles, rows, wide), lambda k: (k, 0, 0, 0)),
            pl.BlockSpec((devices, group, boxes, columns), lambda k: (0, k, 0, 0)),
        ],
        out_specs=pl.BlockSpec((group, rows, columns), lambda k: (k, 0, 0)),
        compiler_params=pltpu.CompilerParams(vmem_limit_bytes=40 * MIB),
        cost_estimate=LITTLE,
        name="near_product",
    )(blocks, slab)


def far_sources(arrived, inner):
    sources = []
    for piece_ref in arrived:
        for slot in range(piece_ref.shape[0]):
            pieces = [piece_ref[slot, piece, inner] for piece in range(piece_ref.shape[1])]
            sources.append(stack_rows(jnp.concatenate(pieces, axis=0)))
    return jnp.concatenate(sources, axis=0)


def far_first(blocks, arrived, before):
    dirs, slots, rows, wide = blocks.shape
    cap, per_tile, _, boxes, columns = arrived[0].shape
    count = len(arrived)
    group = STEP_DIRS if dirs % STEP_DIRS == 0 else 1

    def kernel(block_ref, before_ref, *refs):
        for inner in range(group):
            refs[count][inner] = before_ref[inner] + jnp.dot(
                wide_block(block_ref.at[inner], slots),
                far_sources(refs[:count], inner),
                preferred_element_type=jnp.float32,
            )

    return pl.pallas_call(
        kernel,
        grid=(dirs // group,),
        out_shape=jax.ShapeDtypeStruct((dirs, rows, columns), jnp.float32),
        in_specs=[
            pl.BlockSpec((group, slots, rows, wide), lambda k: (k, 0, 0, 0)),
            pl.BlockSpec((group, rows, columns), lambda k: (k, 0, 0)),
        ]
        + [pl.BlockSpec((cap, per_tile, group, boxes, columns), lambda k: (0, 0, k, 0, 0))] * count,
        out_specs=pl.BlockSpec((group, rows, columns), lambda k: (k, 0, 0)),
        compiler_params=pltpu.CompilerParams(vmem_limit_bytes=40 * MIB),
        cost_estimate=LITTLE,
        name="far_first",
    )(blocks, before, *arrived)


def far_last(blocks, arrived, before, place, devices):
    dirs, slots, rows, wide = blocks.shape
    boxes, columns = arrived.shape[-2:]

    def kernel(place_ref, block_ref, before_ref, arrived_ref, *refs):
        outs, total_ref = refs[:devices], refs[devices]
        for inner in range(dirs):
            total_ref[inner] = before_ref[inner] + jnp.dot(
                wide_block(block_ref.at[inner], slots),
                far_sources([arrived_ref], inner),
                preferred_element_type=jnp.float32,
            )
        for index in range(devices):
            at = pl.multiple_of((place_ref[0] ^ index) * boxes, boxes)
            for inner in range(dirs):
                outs[index][inner] = total_ref[inner, pl.ds(at, boxes), :].astype(jnp.bfloat16)

    return pl.pallas_call(
        kernel,
        out_shape=[jax.ShapeDtypeStruct((dirs, boxes, columns), jnp.bfloat16)] * devices,
        in_specs=smem(1) + vmem(3),
        out_specs=vmem(devices),
        scratch_shapes=[pltpu.VMEM((dirs, rows, columns), jnp.float32)],
        compiler_params=pltpu.CompilerParams(vmem_limit_bytes=20 * MIB),
        cost_estimate=LITTLE,
        name="far_last",
    )(place, blocks, before, arrived)


def disaggregate(returned, disaggregation, place):
    dirs, boxes, columns = returned[0].shape
    devices = len(returned)
    unknowns = disaggregation.shape[0]
    all_dirs = disaggregation.shape[1] // 2
    cuts = OUT_CUTS if boxes % OUT_CUTS == 0 else 1
    size = boxes // cuts

    def kernel(place_ref, dis_ref, *refs):
        out_hbm, scratch, result, sem = refs[devices:]
        for index, other in enumerate(order(devices)):
            first = (place_ref[0] ^ other) * dirs
            for inner in range(dirs):
                at = (first + inner) * (boxes + 1)
                scratch[pl.ds(at, boxes), :] = refs[index][inner].astype(jnp.float32)
        matrix = dis_ref[...]
        copies = []
        for cut in range(cuts):
            for box in range(cut * size, (cut + 1) * size):
                rows = stack_rows(scratch[pl.ds(box, all_dirs, stride=boxes + 1), :])
                result[box] = jnp.dot(matrix, rows, preferred_element_type=jnp.float32).astype(jnp.bfloat16)
            at = pl.ds(cut * size, size)
            copies.append(pltpu.make_async_copy(result.at[at], out_hbm.at[at], sem.at[cut]))
            copies[cut].start()
        for copy in copies:
            copy.wait()

    return pl.pallas_call(
        kernel,
        out_shape=jax.ShapeDtypeStruct((boxes, unknowns, columns), jnp.bfloat16),
        in_specs=smem(1) + vmem(1 + devices),
        out_specs=pl.BlockSpec(memory_space=pl.ANY),
        scratch_shapes=[
            pltpu.VMEM(((all_dirs + 1) * (boxes + 1), columns), jnp.float32),
            pltpu.VMEM((boxes, unknowns, columns), jnp.bfloat16),
            pltpu.SemaphoreType.DMA((cuts,)),
        ],
        compiler_params=pltpu.CompilerParams(vmem_limit_bytes=20 * MIB),
        cost_estimate=LITTLE,
        name="disaggregate",
    )(place, disaggregation, *[returned[other] for other in order(devices)])


def crossed(pieces, axis):
    count = len(pieces)
    moved = [lax.ppermute(pieces[step], axis, [(i, i ^ step) for i in range(count)]) for step in range(1, count)]
    return [pieces[0]] + moved


def make_local(sectors, devices):
    partners = sectors - 1
    barrier = lax.optimization_barrier

    def local(
        fields,
        aggregation,
        operators,
        disaggregation,
        near_tile,
        near_operator,
        far_slot,
        far_operator,
        send_tiles,
    ):
        per_tile = operators.shape[2] // fields.shape[0]
        cap = send_tiles.shape[2]
        where = lax.axis_index("sector").astype(jnp.int32).reshape(1)
        place = lax.axis_index("dir").astype(jnp.int32).reshape(1)
        listing = lax.dynamic_index_in_dim(jnp.swapaxes(send_tiles, 1, 2), where[0], 0, keepdims=False)
        outgoing = list(aggregate(fields, aggregation, place, devices))
        outgoing[0], listing = barrier((outgoing[0], listing))
        pieces = crossed(outgoing, "dir")
        slab, leaving = pick(pieces, listing, where, place, partners, per_tile)
        leaving, tile_index = barrier((leaving, near_tile))
        ranks = sorted(range(1, sectors), key=lambda step: 2 - step if step <= 2 else step - 1)
        arrived = crossed([leaving[0], *leaving], "sector")[1:]
        arrived = [arrived[step - 1] for step in ranks]
        near_blocks, far_blocks, last_blocks = build(
            operators, tile_index, near_operator, far_slot, far_operator, where, partners, cap
        )
        total = near_product(near_blocks, slab, per_tile)
        total = far_first(far_blocks, arrived[:-1], total)
        incoming = far_last(last_blocks, arrived[-1], total, place, devices)
        returned = crossed(incoming, "dir")
        return disaggregate(returned, disaggregation, place)

    return local


def solution(mesh):
    placed = (
        P(("sector", "dir"), None, None),
        P(),
        P(None, "dir", None, None),
        P(),
        P("sector", None),
        P("sector", None),
        P("sector", None),
        P("sector", None),
        P(),
    )
    return jax.shard_map(
        make_local(mesh.shape["sector"], mesh.shape["dir"]),
        mesh=mesh,
        in_specs=placed,
        out_specs=P(("sector", "dir"), None, None),
        check_vma=False,
    )
```

```python
import jax
import jax.numpy as jnp
from jax import lax
from jax.experimental import pallas as pl
from jax.experimental.pallas import tpu as pltpu
from jax.sharding import PartitionSpec as P

MIB = 1024 * 1024
STEP_DIRS = 2
AGG_MIB = 20
OP_CUTS = 4
OUT_CUTS = 8
LITTLE = pl.CostEstimate(flops=1, bytes_accessed=1, transcendentals=0)


def order(count):
    return sorted(range(count), key=lambda step: (step == 0, -bin(step >> 1).count("1"), -(step & 1), step))


def turned(values):
    half = values.shape[-1] // 2
    lane = lax.broadcasted_iota(jnp.int32, values.shape, values.ndim - 1)
    moved = pltpu.roll(values, half, values.ndim - 1)
    return jnp.where(lane < half, -moved, moved)


def stack_rows(values):
    wide = values.astype(jnp.float32)
    return jnp.concatenate([wide, turned(wide)], axis=0).astype(jnp.bfloat16)


def vmem(count):
    return [pl.BlockSpec(memory_space=pltpu.VMEM)] * count


def smem(count):
    return [pl.BlockSpec(memory_space=pltpu.SMEM)] * count


def aggregate(fields, aggregation, place, devices):
    boxes, unknowns, columns = fields.shape
    all_dirs = aggregation.shape[0]
    part = all_dirs // devices

    def kernel(place_ref, fields_ref, agg_ref, *refs):
        outs, scratch = refs[:devices], refs[devices]
        matrix = jnp.concatenate([agg_ref[:, :unknowns], agg_ref[:, unknowns:]], axis=0)
        for box in range(0, boxes, 2):
            pair = jnp.concatenate([fields_ref[box], fields_ref[box + 1]], axis=1)
            wide = jnp.dot(matrix, pair, preferred_element_type=jnp.float32)
            for side in range(2):
                both = wide[:, side * columns : (side + 1) * columns]
                at = pl.ds((box + side) * (all_dirs + 1), all_dirs)
                scratch[at, :] = both[:all_dirs] + turned(both[all_dirs:])
        for step in range(devices):
            first = (place_ref[0] ^ step) * part
            for inner in range(part):
                rows = scratch[pl.ds(first + inner, boxes, stride=all_dirs + 1), :]
                outs[step][inner] = rows.astype(jnp.bfloat16)

    return pl.pallas_call(
        kernel,
        out_shape=[jax.ShapeDtypeStruct((part, boxes, columns), jnp.bfloat16)] * devices,
        in_specs=smem(1) + vmem(2),
        out_specs=vmem(devices),
        scratch_shapes=[pltpu.VMEM(((boxes + 1) * (all_dirs + 1), columns), jnp.float32)],
        compiler_params=pltpu.CompilerParams(vmem_limit_bytes=AGG_MIB * MIB),
        cost_estimate=LITTLE,
        name="aggregate",
    )(place, fields, aggregation)


def pick(pieces, listing, where, place, partners, per_tile):
    devices = len(pieces)
    dirs, boxes, columns = pieces[0].shape
    cap = listing.shape[0]

    def kernel(listing_ref, where_ref, place_ref, *refs):
        slab_ref, outs = refs[devices], refs[devices + 1 :]
        for index, step in enumerate(order(devices)):
            slab_ref[place_ref[0] ^ step] = refs[index][...]
        for index in range(partners):
            other = where_ref[0] ^ (index + 1)
            for slot in range(cap):
                tile = listing_ref[slot, other]
                outs[index][slot] = slab_ref[pl.ds(tile * per_tile, per_tile)]

    shapes = [(devices, dirs, boxes, columns)] + [(cap, per_tile, dirs, boxes, columns)] * partners
    outs = pl.pallas_call(
        kernel,
        out_shape=[jax.ShapeDtypeStruct(shape, jnp.bfloat16) for shape in shapes],
        in_specs=smem(3) + vmem(devices),
        out_specs=vmem(len(shapes)),
        compiler_params=pltpu.CompilerParams(vmem_limit_bytes=20 * MIB),
        cost_estimate=LITTLE,
        name="pick",
    )(listing, where, place, *[pieces[step] for step in order(devices)])
    return outs[0], outs[1:]


def build(operators, near_tile, near_operator, far_slot, far_operator, where, partners, cap):
    count, dirs, rows, wide = operators.shape
    tiles, entries = near_tile.shape
    far_entries = far_slot.shape[1]
    slots = partners * cap
    group = min(4, tiles)
    total = entries + far_entries
    cuts = OP_CUTS if count % OP_CUTS == 0 else 1
    size = count // cuts
    tables = (near_tile, near_operator, far_slot, far_operator)

    def kernel(where_ref, *refs):
        sources, op_hbm, near_out, far_out, last_out = refs[:4], refs[4], refs[5], refs[6], refs[7]
        listed, slot_table, op_table, ops, table_sem, op_sem = refs[8:12], refs[12], refs[13], refs[14], refs[15], refs[16]
        sums = refs[17:]
        near_sum, far_sum = sums[:group], sums[group:]
        now = pl.program_id(0)

        def table_copy(index):
            return pltpu.make_async_copy(sources[index], listed[index], table_sem.at[index])

        def op_copy(direction, cut):
            at = pl.ds(cut * size, size)
            return pltpu.make_async_copy(op_hbm.at[at, direction], ops.at[direction, at], op_sem.at[direction, cut])

        @pl.when(now == 0)
        def _():
            for index in range(4):
                table_copy(index).start()
            for direction in range(dirs):
                for cut in range(cuts):
                    op_copy(direction, cut).start()
            for index in range(4):
                table_copy(index).wait()
            for tile in range(tiles):

                def fill(entry, _):
                    slot_table[tile * total + entry] = listed[0][tile, entry]
                    op_table[tile * total + entry] = listed[1][tile, entry]
                    return 0

                def fill_far(entry, _):
                    place = listed[2][tile, entry]
                    sector = lax.div(place, cap)
                    step = sector ^ where_ref[0]
                    slot = (jnp.where(step <= 2, 2 - step, step - 1)) * cap + place - sector * cap
                    slot_table[tile * total + entries + entry] = slot
                    op_table[tile * total + entries + entry] = listed[3][tile, entry]
                    return 0

                lax.fori_loop(0, entries, fill, 0, unroll=4)
                lax.fori_loop(0, far_entries, fill_far, 0, unroll=4)

        for cut in range(cuts):
            op_copy(now, cut).wait()
        for base in range(0, tiles, group):
            for ref in sums:
                ref[...] = jnp.zeros_like(ref)
            for entry in range(total):
                for t in range(group):
                    at = (base + t) * total + entry
                    kept = near_sum[t] if entry < entries else far_sum[t]
                    kept[slot_table[at]] += ops[now, op_table[at]].astype(jnp.float32)
            for t in range(group):
                at = pl.ds((base + t) * rows, rows)
                near_out[:, at, :] = near_sum[t][...].astype(jnp.bfloat16)
                far_out[:, at, :] = far_sum[t][: slots - cap].astype(jnp.bfloat16)
                last_out[:, at, :] = far_sum[t][slots - cap :].astype(jnp.bfloat16)

    need = 2 * operators.size + 4 * group * (tiles + slots) * rows * wide + 8 * (tiles + slots) * tiles * rows * wide
    return pl.pallas_call(
        kernel,
        grid=(dirs,),
        out_shape=[
            jax.ShapeDtypeStruct((dirs, tiles, tiles * rows, wide), jnp.bfloat16),
            jax.ShapeDtypeStruct((dirs, slots - cap, tiles * rows, wide), jnp.bfloat16),
            jax.ShapeDtypeStruct((dirs, cap, tiles * rows, wide), jnp.bfloat16),
        ],
        in_specs=smem(1) + [pl.BlockSpec(memory_space=pltpu.HBM)] * 5,
        out_specs=[
            pl.BlockSpec((None, tiles, tiles * rows, wide), lambda k: (k, 0, 0, 0)),
            pl.BlockSpec((None, slots - cap, tiles * rows, wide), lambda k: (k, 0, 0, 0)),
            pl.BlockSpec((None, cap, tiles * rows, wide), lambda k: (k, 0, 0, 0)),
        ],
        scratch_shapes=[pltpu.SMEM(table.shape, jnp.int32) for table in tables]
        + [pltpu.SMEM((tiles * total,), jnp.int32)] * 2
        + [
            pltpu.VMEM((dirs, count, rows, wide), jnp.bfloat16),
            pltpu.SemaphoreType.DMA((4,)),
            pltpu.SemaphoreType.DMA((dirs, cuts)),
        ]
        + [pltpu.VMEM((tiles, rows, wide), jnp.float32)] * group
        + [pltpu.VMEM((slots, rows, wide), jnp.float32)] * group,
        compiler_params=pltpu.CompilerParams(vmem_limit_bytes=need + 4 * MIB),
        cost_estimate=LITTLE,
        name="build",
    )(where, *tables, operators)


def wide_block(block_ref, slots):
    return jnp.concatenate([block_ref[slot] for slot in range(slots)], axis=1)


def near_product(blocks, slab, per_tile):
    dirs, tiles, rows, wide = blocks.shape
    devices, _, boxes, columns = slab.shape
    group = STEP_DIRS if dirs % STEP_DIRS == 0 else 1

    def kernel(block_ref, slab_ref, out_ref):
        for inner in range(group):
            sources = []
            for tile in range(tiles):
                pieces = [slab_ref[tile * per_tile + piece, inner] for piece in range(per_tile)]
                sources.append(stack_rows(jnp.concatenate(pieces, axis=0)))
            out_ref[inner] = jnp.dot(
                wide_block(block_ref.at[inner], tiles),
                jnp.concatenate(sources, axis=0),
                preferred_element_type=jnp.float32,
            )

    return pl.pallas_call(
        kernel,
        grid=(dirs // group,),
        out_shape=jax.ShapeDtypeStruct((dirs, rows, columns), jnp.float32),
        in_specs=[
            pl.BlockSpec((group, tiles, rows, wide), lambda k: (k, 0, 0, 0)),
            pl.BlockSpec((devices, group, boxes, columns), lambda k: (0, k, 0, 0)),
        ],
        out_specs=pl.BlockSpec((group, rows, columns), lambda k: (k, 0, 0)),
        compiler_params=pltpu.CompilerParams(vmem_limit_bytes=40 * MIB),
        cost_estimate=LITTLE,
        name="near_product",
    )(blocks, slab)


def far_sources(arrived, inner):
    sources = []
    for piece_ref in arrived:
        for slot in range(piece_ref.shape[0]):
            pieces = [piece_ref[slot, piece, inner] for piece in range(piece_ref.shape[1])]
            sources.append(stack_rows(jnp.concatenate(pieces, axis=0)))
    return jnp.concatenate(sources, axis=0)


def far_first(blocks, arrived, before):
    dirs, slots, rows, wide = blocks.shape
    cap, per_tile, _, boxes, columns = arrived[0].shape
    count = len(arrived)
    group = STEP_DIRS if dirs % STEP_DIRS == 0 else 1

    def kernel(block_ref, before_ref, *refs):
        for inner in range(group):
            refs[count][inner] = before_ref[inner] + jnp.dot(
                wide_block(block_ref.at[inner], slots),
                far_sources(refs[:count], inner),
                preferred_element_type=jnp.float32,
            )

    return pl.pallas_call(
        kernel,
        grid=(dirs // group,),
        out_shape=jax.ShapeDtypeStruct((dirs, rows, columns), jnp.float32),
        in_specs=[
            pl.BlockSpec((group, slots, rows, wide), lambda k: (k, 0, 0, 0)),
            pl.BlockSpec((group, rows, columns), lambda k: (k, 0, 0)),
        ]
        + [pl.BlockSpec((cap, per_tile, group, boxes, columns), lambda k: (0, 0, k, 0, 0))] * count,
        out_specs=pl.BlockSpec((group, rows, columns), lambda k: (k, 0, 0)),
        compiler_params=pltpu.CompilerParams(vmem_limit_bytes=40 * MIB),
        cost_estimate=LITTLE,
        name="far_first",
    )(blocks, before, *arrived)


def far_last(blocks, arrived, before, place, devices):
    dirs, slots, rows, wide = blocks.shape
    boxes, columns = arrived.shape[-2:]

    def kernel(place_ref, block_ref, before_ref, arrived_ref, *refs):
        outs, total_ref = refs[:devices], refs[devices]
        for inner in range(dirs):
            total_ref[inner] = before_ref[inner] + jnp.dot(
                wide_block(block_ref.at[inner], slots),
                far_sources([arrived_ref], inner),
                preferred_element_type=jnp.float32,
            )
        for index in range(devices):
            at = pl.multiple_of((place_ref[0] ^ index) * boxes, boxes)
            for inner in range(dirs):
                outs[index][inner] = total_ref[inner, pl.ds(at, boxes), :].astype(jnp.bfloat16)

    return pl.pallas_call(
        kernel,
        out_shape=[jax.ShapeDtypeStruct((dirs, boxes, columns), jnp.bfloat16)] * devices,
        in_specs=smem(1) + vmem(3),
        out_specs=vmem(devices),
        scratch_shapes=[pltpu.VMEM((dirs, rows, columns), jnp.float32)],
        compiler_params=pltpu.CompilerParams(vmem_limit_bytes=20 * MIB),
        cost_estimate=LITTLE,
        name="far_last",
    )(place, blocks, before, arrived)


def disaggregate(returned, disaggregation, place):
    dirs, boxes, columns = returned[0].shape
    devices = len(returned)
    unknowns = disaggregation.shape[0]
    all_dirs = disaggregation.shape[1] // 2
    cuts = OUT_CUTS if boxes % OUT_CUTS == 0 else 1
    size = boxes // cuts

    def kernel(place_ref, dis_ref, *refs):
        out_hbm, scratch, result, sem = refs[devices:]
        for index, other in enumerate(order(devices)):
            first = (place_ref[0] ^ other) * dirs
            for inner in range(dirs):
                at = (first + inner) * (boxes + 1)
                scratch[pl.ds(at, boxes), :] = refs[index][inner].astype(jnp.float32)
        matrix = dis_ref[...]
        copies = []
        for cut in range(cuts):
            for box in range(cut * size, (cut + 1) * size, 2):
                rows = [stack_rows(scratch[pl.ds(box + side, all_dirs, stride=boxes + 1), :]) for side in range(2)]
                both = jnp.dot(matrix, jnp.concatenate(rows, axis=1), preferred_element_type=jnp.float32)
                for side in range(2):
                    result[box + side] = both[:, side * columns : (side + 1) * columns].astype(jnp.bfloat16)
            at = pl.ds(cut * size, size)
            copies.append(pltpu.make_async_copy(result.at[at], out_hbm.at[at], sem.at[cut]))
            copies[cut].start()
        for copy in copies:
            copy.wait()

    return pl.pallas_call(
        kernel,
        out_shape=jax.ShapeDtypeStruct((boxes, unknowns, columns), jnp.bfloat16),
        in_specs=smem(1) + vmem(1 + devices),
        out_specs=pl.BlockSpec(memory_space=pl.ANY),
        scratch_shapes=[
            pltpu.VMEM(((all_dirs + 1) * (boxes + 1), columns), jnp.float32),
            pltpu.VMEM((boxes, unknowns, columns), jnp.bfloat16),
            pltpu.SemaphoreType.DMA((cuts,)),
        ],
        compiler_params=pltpu.CompilerParams(vmem_limit_bytes=20 * MIB),
        cost_estimate=LITTLE,
        name="disaggregate",
    )(place, disaggregation, *[returned[other] for other in order(devices)])


def crossed(pieces, axis):
    count = len(pieces)
    moved = [lax.ppermute(pieces[step], axis, [(i, i ^ step) for i in range(count)]) for step in range(1, count)]
    return [pieces[0]] + moved


def make_local(sectors, devices):
    partners = sectors - 1
    barrier = lax.optimization_barrier

    def local(
        fields,
        aggregation,
        operators,
        disaggregation,
        near_tile,
        near_operator,
        far_slot,
        far_operator,
        send_tiles,
    ):
        per_tile = operators.shape[2] // fields.shape[0]
        cap = send_tiles.shape[2]
        where = lax.axis_index("sector").astype(jnp.int32).reshape(1)
        place = lax.axis_index("dir").astype(jnp.int32).reshape(1)
        listing = lax.dynamic_index_in_dim(jnp.swapaxes(send_tiles, 1, 2), where[0], 0, keepdims=False)
        outgoing = list(aggregate(fields, aggregation, place, devices))
        outgoing[0], listing = barrier((outgoing[0], listing))
        pieces = crossed(outgoing, "dir")
        slab, leaving = pick(pieces, listing, where, place, partners, per_tile)
        leaving, tile_index = barrier((leaving, near_tile))
        ranks = sorted(range(1, sectors), key=lambda step: 2 - step if step <= 2 else step - 1)
        arrived = crossed([leaving[0], *leaving], "sector")[1:]
        arrived = [arrived[step - 1] for step in ranks]
        near_blocks, far_blocks, last_blocks = build(
            operators, tile_index, near_operator, far_slot, far_operator, where, partners, cap
        )
        total = near_product(near_blocks, slab, per_tile)
        total = far_first(far_blocks, arrived[:-1], total)
        incoming = far_last(last_blocks, arrived[-1], total, place, devices)
        returned = crossed(incoming, "dir")
        return disaggregate(returned, disaggregation, place)

    return local


def solution(mesh):
    placed = (
        P(("sector", "dir"), None, None),
        P(),
        P(None, "dir", None, None),
        P(),
        P("sector", None),
        P("sector", None),
        P("sector", None),
        P("sector", None),
        P(),
    )
    return jax.shard_map(
        make_local(mesh.shape["sector"], mesh.shape["dir"]),
        mesh=mesh,
        in_specs=placed,
        out_specs=P(("sector", "dir"), None, None),
        check_vma=False,
    )
```
